32 devices in a mesh: ctx: 16 (over z, y, core), fsdp: 2 (over x).
Axes of the slice: x: 2, y: 2, z: 4, core: 2. Of those that a mesh axis runs over, the one named last changes fastest.
Arguments:
- inputs: bfloat16 [2, 2048, 1024], P('fsdp', 'ctx'), may hold values from -6 to 6
- cotangent: bfloat16 [2, 2048, 1024], P('fsdp', 'ctx'), may hold values from -6 to 6
- lengths: int32 [2, 4], P('fsdp'), may hold values from 1 to 1984, 2048 in all within a row
- order: int32 [2, 16, 16], P('fsdp'), may hold values from 0 to 15, each once within a row
- pad_mask: int32 [2, 2048], P('fsdp', 'ctx'), may hold values 0 or 1
- attn_weights: float32 [1024, 3072], P(('ctx', 'fsdp'))
- attn_first: float32 [1024, 3072], P(('ctx', 'fsdp'))
- attn_second: float32 [1024, 3072], P(('ctx', 'fsdp'))
- ffn_weights: float32 [4608, 3072], P(('ctx', 'fsdp'))
- ffn_first: float32 [4608, 3072], P(('ctx', 'fsdp'))
- ffn_second: float32 [4608, 3072], P(('ctx', 'fsdp'))
- gains: float32 [2176], replicated, may hold values from 0.7 to 1.6
- gain_first: float32 [2176], replicated
- gain_second: float32 [2176], replicated
Outputs:
- output: float32 [2, 2048, 1024], P('fsdp', 'ctx')
- input_grad: float32 [2, 2048, 1024], P('fsdp', 'ctx')
- attn_grad: float32 [1024, 3072], P(('ctx', 'fsdp'))
- attn_second_new: float32 [1024, 3072], P(('ctx', 'fsdp'))
- attn_new: float32 [1024, 3072], P(('ctx', 'fsdp'))
- ffn_grad: float32 [4608, 3072], P(('ctx', 'fsdp'))
- ffn_second_new: float32 [4608, 3072], P(('ctx', 'fsdp'))
- ffn_new: float32 [4608, 3072], P(('ctx', 'fsdp'))
- gain_grad: float32 [2176], replicated
- gain_second_new: float32 [2176], replicated
- gain_new: float32 [2176], replicated
The draws below stay inside these ranges and needn't reach their ends.
Inputs may be any that keep to these rules, and one draw needn't show every extreme that they name: In each micro-batch the 4 lengths add up to 2048, and the longest is exactly 1984. For each micro-batch m and each index j along ctx, order[m, j, :] holds every index along ctx once: the device at index e holds, as its j-th run of 8 rows, run order[m, j, e] of the 128 tokens that follow token j * 128 in sequence order.
All inputs are finite; a program needn't handle non-finite values. No bound on the sum of `pad_mask` on one device may be relied on, other than what follows from the above.
Results may differ from the reference program's by a relative error of at most 0.015.
Values may be sent and summed in bfloat16 or wider, within the bound.
No kernel may reach another device: no remote copies, remote signals or barrier semaphores. Data moves between devices by JAX's collectives and lax.ppermute only.
A program may use at most 576 MiB of HBM per device.

```python
import math
import jax
import jax.numpy as jnp
import numpy as np
from jax import lax

D = 1024
QUERY_HEADS = 16
KEY_VALUE_HEADS = 8
HEAD_SIZE = 64
FF = 4608
TOK_DEV = 128
NSEQ = 4
STEP = 10
MB = 2
SEQ_TOK = 2048
GAINS = 2176
N_CTX = 16


def grad_scale():
    return math.sqrt(0.875 * MB * SEQ_TOK)


def column_scales(factors, widths):
    return jnp.concatenate([jnp.full((width_now,), factor, jnp.float32) for factor, width_now in zip(factors, widths)])


def attention_widths():
    return [QUERY_HEADS * HEAD_SIZE, KEY_VALUE_HEADS * HEAD_SIZE, KEY_VALUE_HEADS * HEAD_SIZE, QUERY_HEADS * HEAD_SIZE]


def ffn_widths():
    return [D, D, D]


def draw_attn_weights(key, part):
    key = jax.random.fold_in(key, 11)
    columns = column_scales([D ** (-0.5), D ** (-0.5), D ** (-0.5), (QUERY_HEADS * HEAD_SIZE / 16.0) ** (-0.5)], attention_widths())
    array_shape = (D, columns.shape[0])
    raw_draw = jax.random.normal(key, array_shape, jnp.float32)
    return raw_draw * columns[None, :]


def draw_attn_first(key, part):
    key = jax.random.fold_in(key, 12)
    columns = column_scales([0.5, 0.8, 0.5, 0.2], attention_widths()) * (0.1111 * grad_scale())
    array_shape = (D, columns.shape[0])
    raw_draw = jax.random.normal(key, array_shape, jnp.float32)
    return raw_draw * columns[None, :]


def draw_attn_second(key, part):
    key = jax.random.fold_in(key, 13)
    columns = column_scales([0.5, 0.8, 0.5, 0.2], attention_widths()) * grad_scale()
    array_shape = (D, columns.shape[0])
    factor_draw = jnp.exp(jax.random.uniform(key, array_shape, jnp.float32, 0.0, math.log(4.0)))
    return factor_draw * (0.001001 * columns * columns)[None, :]


def draw_ffn_weights(key, part):
    key = jax.random.fold_in(key, 21)
    columns = column_scales([D ** (-0.5), D ** (-0.5), FF ** (-0.5)], ffn_widths())
    array_shape = (FF, 3 * D)
    raw_draw = jax.random.normal(key, array_shape, jnp.float32)
    return raw_draw * columns[None, :]


def draw_ffn_first(key, part):
    key = jax.random.fold_in(key, 22)
    columns = column_scales([0.25, 0.25, 0.6], ffn_widths()) * (0.1111 * grad_scale())
    array_shape = (FF, 3 * D)
    raw_draw = jax.random.normal(key, array_shape, jnp.float32)
    return raw_draw * columns[None, :]


def draw_ffn_second(key, part):
    key = jax.random.fold_in(key, 23)
    columns = column_scales([0.25, 0.25, 0.6], ffn_widths()) * grad_scale()
    array_shape = (FF, 3 * D)
    factor_draw = jnp.exp(jax.random.uniform(key, array_shape, jnp.float32, 0.0, math.log(4.0)))
    return factor_draw * (0.001001 * columns * columns)[None, :]


def draw_gain_first(key, part):
    key = jax.random.fold_in(key, 31)
    array_shape = (2 * D + 2 * HEAD_SIZE,)
    raw_draw = jax.random.normal(key, array_shape, jnp.float32)
    return raw_draw * (0.1111 * 2.0 * grad_scale())


def draw_gain_second(key, part):
    key = jax.random.fold_in(key, 32)
    array_shape = (2 * D + 2 * HEAD_SIZE,)
    factor_draw = jnp.exp(jax.random.uniform(key, array_shape, jnp.float32, 0.0, math.log(4.0)))
    return factor_draw * (0.001001 * 4.0 * grad_scale() * grad_scale())


def place_ends(array, own_key, least, top_value):
    longest = array.shape.index(max(array.shape))
    spots = []
    for shift in (0, 1):
        where = [jax.random.randint(jax.random.fold_in(own_key, axis), (), 0, length) for axis, length in enumerate(array.shape)]
        where[longest] = (where[longest] + shift) % array.shape[longest]
        spots.append(tuple(where))
    return array.at[spots[0]].set(least).at[spots[1]].set(top_value)


def level_of(stream_key, shape, split, least, top_value):
    def one(axis_at, parts):
        steps = jax.random.uniform(jax.random.fold_in(jax.random.fold_in(stream_key, 6), axis_at), (parts,), jnp.float32, least / len(split), top_value / len(split))
        return jnp.repeat(jnp.exp(steps), shape[axis_at] // parts).reshape((-1,) + (1,) * (len(shape) - axis_at - 1))

    level = one(*split[0])
    for cut in split[1:]:
        level = level * one(*cut)
    return level


def profile(amount, total, reach, lean):
    portions = [(1 << 20) // math.isqrt(standing ** lean) + 1 for standing in range(2, amount + 1)]
    rest, given = total - reach - (amount - 1), [1] * (amount - 1)
    while rest > 0:
        movable = [i for i in range(amount - 1) if given[i] < reach]
        whole, budget = sum([portions[i] for i in movable]), rest
        for i in movable:
            more = min(reach - given[i], max(1, budget * portions[i] // whole), rest)
            given[i] = given[i] + more
            rest = rest - more
    return np.array([reach] + given)


def uneven(key, number_of, total, reach, skew):
    if number_of == 2:
        one = jax.random.randint(key, (), max(1, total - reach), min(reach, total - 1) + 1)
        return jnp.stack([one, total - one])
    sizes = jnp.asarray(profile(number_of, total, reach, skew), jnp.int32)
    twos = (number_of - 1) // 2
    giver, taker = sizes[1:1 + 2 * twos:2], sizes[2:2 + 2 * twos:2]
    slack = jnp.minimum(giver - 1, reach - taker)
    moved = jax.random.randint(jax.random.fold_in(key, 1), (twos,), 0, 1 << 20) % (slack + 1)
    sizes = sizes.at[1:1 + 2 * twos:2].set(giver - moved).at[2:2 + 2 * twos:2].set(taker + moved)
    return sizes[jax.random.permutation(jax.random.fold_in(key, 2), number_of)]


def scatter_about(rng, extent, deviation, most, pieces=(), kind=jnp.bfloat16):
    loudness = level_of(rng, extent, pieces, -0.22, 0.18) if pieces else 1.0
    drawn = jax.random.normal(rng, extent, jnp.float32) * deviation * loudness
    return jnp.minimum(jnp.maximum(drawn, -most), most).astype(kind)


def setup_inputs(seed: int = 0) -> dict:
    key_list = jax.random.split(jax.random.key(seed), 15)
    return {
        "inputs": scatter_about(key_list[0], (MB, SEQ_TOK, D), 1.0, 6.0, ((0, 2), (1, 16))),
        "cotangent": scatter_about(key_list[1], (MB, SEQ_TOK, D), 1.0, 6.0, ((0, 2), (1, 16))),
        "lengths": jax.vmap(lambda own: uneven(own, NSEQ, SEQ_TOK, SEQ_TOK - TOK_DEV // 2, 2))(jax.random.split(key_list[2], MB)).reshape((MB, NSEQ)).astype(jnp.int32),
        "order": jax.vmap(lambda own: jax.random.permutation(own, N_CTX))(jax.random.split(key_list[3], MB * N_CTX)).reshape((MB, N_CTX, N_CTX)).astype(jnp.int32),
        "pad_mask": place_ends((jax.random.randint(key_list[4], (MB, SEQ_TOK), 0, 8) < 7).astype(jnp.int32), jax.random.fold_in(key_list[4], 1), 0, 1),
        "attn_weights": draw_attn_weights(jax.random.fold_in(key_list[14], 71), 0),
        "attn_first": draw_attn_first(jax.random.fold_in(key_list[14], 71), 0),
        "attn_second": draw_attn_second(jax.random.fold_in(key_list[14], 71), 0),
        "ffn_weights": draw_ffn_weights(jax.random.fold_in(key_list[14], 71), 0),
        "ffn_first": draw_ffn_first(jax.random.fold_in(key_list[14], 71), 0),
        "ffn_second": draw_ffn_second(jax.random.fold_in(key_list[14], 71), 0),
        "gains": jnp.clip(jax.random.uniform(key_list[11], (GAINS,), jnp.float32, 0.7, 1.6), 0.7, 1.6),
        "gain_first": draw_gain_first(jax.random.fold_in(key_list[14], 71), 0),
        "gain_second": draw_gain_second(jax.random.fold_in(key_list[14], 71), 0),
    }


EPSILON = 1e-05
ROPE_BASE = 1000000.0
SHIFT_FACTOR = 2.6
QUERY_BLOCK = 512
BETA_FIRST = 0.9
BETA_SECOND = 0.999
ADAM_EPSILON = 1e-08
WEIGHT_DECAY = 0.01
GAIN_RATE = 0.8
HIGHEST = lax.Precision.HIGHEST

@jax.custom_vjp
def reduced_precision(v):
    return lax.optimization_barrier(v.astype(jnp.bfloat16)).astype(jnp.float32)

@jax.custom_vjp
def low_back(v):
    return v

def low_keep(v):
    return (reduced_precision(v), None)

def low_pass(kept, grad):
    return (grad,)

def back_keep(v):
    return (v, None)

def back_low(kept, grad):
    return (reduced_precision(grad),)
reduced_precision.defvjp(low_keep, low_pass)
low_back.defvjp(back_keep, back_low)

def placed_tokens(order_table):
    devices = order_table.shape[0]
    piece_rows = TOK_DEV // devices
    slot_index = jnp.arange(devices, dtype=jnp.int32)
    inside = jnp.arange(piece_rows, dtype=jnp.int32)
    token_grid = slot_index[None, :, None] * TOK_DEV + jnp.transpose(order_table)[:, :, None] * piece_rows + inside[None, None, :]
    return token_grid.reshape(-1).astype(jnp.int32)

def sequence_info(token_inputs, lengths):
    seq_ends = jnp.cumsum(lengths).astype(jnp.int32)
    begins = (seq_ends - lengths).astype(jnp.int32)
    segment_ids = lax.optimization_barrier(jnp.sum((token_inputs[:, None] >= seq_ends[None, :]).astype(jnp.int32), axis=1)).astype(jnp.int32)
    chosen = segment_ids[:, None] == jnp.arange(lengths.shape[0], dtype=jnp.int32)[None, :]
    seq_first = lax.optimization_barrier(jnp.sum(jnp.where(chosen, begins[None, :], 0), axis=1)).astype(jnp.int32)
    return (segment_ids, token_inputs - seq_first)

def rotation(position):
    half_width = HEAD_SIZE // 2
    frequency = jnp.exp(jnp.arange(half_width, dtype=jnp.float32) * (-2.0 * math.log(ROPE_BASE) / HEAD_SIZE))
    angles = position.astype(jnp.float32)[:, None] * frequency[None, :]
    return (jnp.cos(angles), jnp.sin(angles))

def rotary_apply(values, cosine_table, sine_table):
    half_width = values.shape[-1] // 2
    front = values[..., :half_width]
    second_half = values[..., half_width:]
    cosine_wide = cosine_table[:, None, :]
    sine_wide = sine_table[:, None, :]
    return jnp.concatenate([front * cosine_wide - second_half * sine_wide, second_half * cosine_wide + front * sine_wide], axis=-1)

def norm_per_head(values, gain_row):
    return values * lax.rsqrt(lax.optimization_barrier(jnp.mean(values * values, axis=-1, keepdims=True)) + EPSILON) * gain_row

def attention_apply(query_tensor, key_tensor, values, segment_ids, token_inputs):
    length_total = query_tensor.shape[0]
    scale = HEAD_SIZE ** (-0.5)
    shift = SHIFT_FACTOR * HEAD_SIZE ** 0.5

    def one_block(number):
        offset = (number * QUERY_BLOCK).astype(jnp.int32)
        query_rows = lax.dynamic_slice_in_dim(query_tensor, offset, QUERY_BLOCK, 0)
        query_segment = lax.dynamic_slice_in_dim(segment_ids, offset, QUERY_BLOCK, 0)
        query_tokens = lax.dynamic_slice_in_dim(token_inputs, offset, QUERY_BLOCK, 0)
        visible = (query_segment[:, None] == segment_ids[None, :]) & (token_inputs[None, :] <= query_tokens[:, None])
        scores = low_back(jnp.einsum('rkgd,ckd->kgrc', query_rows, key_tensor, precision=HIGHEST) * scale)
        weight = jnp.where(visible[None, None], jnp.exp(scores - shift), 0.0)
        totals = lax.optimization_barrier(jnp.sum(weight, axis=-1))
        numer = low_back(jnp.einsum('kgrc,ckd->rkgd', reduced_precision(weight), values, precision=HIGHEST))
        return numer / jnp.transpose(totals, (2, 0, 1))[..., None]
    blocks = lax.map(jax.checkpoint(one_block), jnp.arange(length_total // QUERY_BLOCK, dtype=jnp.int32))
    return blocks.reshape(length_total, QUERY_HEADS * HEAD_SIZE)

def block_forward(inputs_f, attn_f, ffn_f, gains_f, cosine_table, sine_table, segment_ids, token_inputs):
    query_width = QUERY_HEADS * HEAD_SIZE
    key_value_width = KEY_VALUE_HEADS * HEAD_SIZE
    query_groups = QUERY_HEADS // KEY_VALUE_HEADS
    length_total = inputs_f.shape[0]
    norm_in = gains_f[:D]
    norm_mid = gains_f[D:2 * D]
    query_gain = gains_f[2 * D:2 * D + HEAD_SIZE]
    key_norm_gain = gains_f[2 * D + HEAD_SIZE:]
    attn_low = reduced_precision(attn_f)
    ffn_low = reduced_precision(ffn_f)
    normed = reduced_precision(inputs_f * lax.rsqrt(lax.optimization_barrier(jnp.mean(inputs_f * inputs_f, axis=-1, keepdims=True)) + EPSILON) * norm_in)
    query_lin = low_back(jnp.dot(normed, attn_low[:, :query_width], precision=HIGHEST))
    key_linear = low_back(jnp.dot(normed, attn_low[:, query_width:query_width + key_value_width], precision=HIGHEST))
    value_linear = reduced_precision(low_back(jnp.dot(normed, attn_low[:, query_width + key_value_width:query_width + 2 * key_value_width], precision=HIGHEST)))
    query_tensor = reduced_precision(rotary_apply(norm_per_head(query_lin.reshape(length_total, QUERY_HEADS, HEAD_SIZE), query_gain), cosine_table, sine_table))
    key_tensor = reduced_precision(rotary_apply(norm_per_head(key_linear.reshape(length_total, KEY_VALUE_HEADS, HEAD_SIZE), key_norm_gain), cosine_table, sine_table))
    combined_heads = attention_apply(query_tensor.reshape(length_total, KEY_VALUE_HEADS, query_groups, HEAD_SIZE), key_tensor, value_linear.reshape(length_total, KEY_VALUE_HEADS, HEAD_SIZE), segment_ids, token_inputs)
    mixed_low = reduced_precision(low_back(combined_heads))
    attn_out = low_back(jnp.dot(mixed_low, attn_low[:, query_width + 2 * key_value_width:].T, precision=HIGHEST))
    hidden = inputs_f + attn_out
    normed_mid = reduced_precision(hidden * lax.rsqrt(lax.optimization_barrier(jnp.mean(hidden * hidden, axis=-1, keepdims=True)) + EPSILON) * norm_mid)
    gate_vals = low_back(jnp.dot(normed_mid, ffn_low[:, :D].T, precision=HIGHEST))
    up_vals = low_back(jnp.dot(normed_mid, ffn_low[:, D:2 * D].T, precision=HIGHEST))
    active = reduced_precision(gate_vals * jax.nn.sigmoid(gate_vals) * up_vals)
    return hidden + jnp.dot(active, ffn_low[:, 2 * D:], precision=HIGHEST)

def attention_rates():
    query_width = QUERY_HEADS * HEAD_SIZE
    key_value_width = KEY_VALUE_HEADS * HEAD_SIZE
    return jnp.concatenate([jnp.full((query_width + 2 * key_value_width,), D ** (-0.5), jnp.float32), jnp.full((query_width,), (query_width / 16.0) ** (-0.5), jnp.float32)])

def ffn_rates():
    return jnp.concatenate([jnp.full((2 * D,), D ** (-0.5), jnp.float32), jnp.full((D,), FF ** (-0.5), jnp.float32)])

def adam_update(weight, gradient, first_moment, second, step_rate):
    first_new = BETA_FIRST * first_moment + (1.0 - BETA_FIRST) * gradient
    second_new = BETA_SECOND * second + (1.0 - BETA_SECOND) * gradient * gradient
    normalized = first_new / (1.0 - BETA_FIRST ** STEP) / (jnp.sqrt(second_new / (1.0 - BETA_SECOND ** STEP)) + ADAM_EPSILON)
    return (weight - step_rate * (normalized + WEIGHT_DECAY * weight), second_new)

def reference(inputs, cotangent, lengths, order, pad_mask, attn_weights, attn_first, attn_second, ffn_weights, ffn_first, ffn_second, gains, gain_first, gain_second):
    total_rows = inputs.shape[1]
    token_inputs = jnp.arange(total_rows, dtype=jnp.int32)

    def micro_step(grad_sums, micro_batch):
        rows_in, back_in, length_row, order_table, keep_rows = micro_batch
        placed = placed_tokens(order_table)
        inverse = jnp.zeros((total_rows,), jnp.int32).at[placed].set(token_inputs)
        ordered = jnp.take(rows_in, inverse, axis=0).astype(jnp.float32)
        segment_ids, position = sequence_info(token_inputs, length_row)
        cosine_table, sine_table = rotation(position)

        def forward(inputs_f, attn_f, ffn_f, gains_f):
            return block_forward(inputs_f, attn_f, ffn_f, gains_f, cosine_table, sine_table, segment_ids, token_inputs)
        result, pullback = jax.vjp(forward, ordered, attn_weights, ffn_weights, gains)
        seed_grad = back_in.astype(jnp.float32) * keep_rows[:, None].astype(jnp.float32)
        grad_input, grad_attention, grad_ffn, grad_gains = pullback(seed_grad)
        new_sums = (grad_sums[0] + grad_attention, grad_sums[1] + grad_ffn, grad_sums[2] + grad_gains)
        return (new_sums, (result, grad_input))
    zero_sums = (jnp.zeros_like(attn_weights), jnp.zeros_like(ffn_weights), jnp.zeros_like(gains))
    grad_sums, results = lax.scan(micro_step, zero_sums, (inputs, cotangent, lengths, order, pad_mask))
    attn_new, attn_second_new = adam_update(attn_weights, grad_sums[0], attn_first, attn_second, attention_rates()[None, :])
    ffn_new, ffn_second_new = adam_update(ffn_weights, grad_sums[1], ffn_first, ffn_second, ffn_rates()[None, :])
    gain_new, gain_second_new = adam_update(gains, grad_sums[2], gain_first, gain_second, GAIN_RATE)
    return (results[0], results[1], grad_sums[0], attn_second_new, attn_new, grad_sums[1], ffn_second_new, ffn_new, grad_sums[2], gain_second_new, gain_new)
```

```python
import functools
import math

import jax
import jax.numpy as jnp
import numpy as np
from jax import lax
from jax.experimental import pallas as pl
from jax.experimental.pallas import tpu as pltpu
from jax.sharding import Mesh, PartitionSpec as P

D = 1024
QUERY_HEADS = 16
KEY_VALUE_HEADS = 8
HEAD_SIZE = 64
FF = 4608
STEP = 10

QUERY_WIDTH = QUERY_HEADS * HEAD_SIZE
KEY_WIDTH = KEY_VALUE_HEADS * HEAD_SIZE
GROUP = QUERY_HEADS // KEY_VALUE_HEADS
PAIR = GROUP * HEAD_SIZE
HEAD_COLS = PAIR + 2 * HEAD_SIZE

EPSILON = 1e-05
ROPE_BASE = 1000000.0
SHIFT_FACTOR = 2.6
SCALE = HEAD_SIZE ** (-0.5)
SHIFT = SHIFT_FACTOR * HEAD_SIZE**0.5
LOG2E = math.log2(math.e)
BETA_FIRST = 0.9
BETA_SECOND = 0.999
ADAM_EPSILON = 1e-08
WEIGHT_DECAY = 0.01
GAIN_RATE = 0.8

BF16 = jnp.bfloat16
F32 = jnp.float32
I32 = jnp.int32
MIB = 1 << 20

def mm(left, right, left_dim, right_dim):
    return lax.dot_general(
        left, right, (((left_dim,), (right_dim,)), ((), ())), preferred_element_type=F32
    )


def rms_parts(values):
    factor = lax.rsqrt(jnp.mean(values * values, axis=-1, keepdims=True) + EPSILON)
    return (factor, values * factor)


def norm_back(grad_hat, unit_vals, factor):
    return factor * (grad_hat - unit_vals * jnp.mean(grad_hat * unit_vals, axis=-1, keepdims=True))


def attention_rates():
    return np.concatenate(
        [
            np.full((QUERY_WIDTH + 2 * KEY_WIDTH,), D ** (-0.5), np.float32),
            np.full((QUERY_WIDTH,), (QUERY_WIDTH / 16.0) ** (-0.5), np.float32),
        ]
    )


def ffn_rates():
    return np.concatenate(
        [np.full((2 * D,), D ** (-0.5), np.float32), np.full((D,), FF ** (-0.5), np.float32)]
    )


def adam_update(weight, gradient, first_moment, second, step_rate):
    first_new = BETA_FIRST * first_moment + (1.0 - BETA_FIRST) * gradient
    second_new = BETA_SECOND * second + (1.0 - BETA_SECOND) * gradient * gradient
    normalized = (
        first_new
        / (1.0 - BETA_FIRST**STEP)
        / (jnp.sqrt(second_new / (1.0 - BETA_SECOND**STEP)) + ADAM_EPSILON)
    )
    return (weight - step_rate * (normalized + WEIGHT_DECAY * weight), second_new)


RINGS = 4
SLOTS = 2 * RINGS
ALL = ("zz", "tt", "core", "fsdp")
CTX = ("zz", "tt", "core")
SLOT, ZZ, TT, CORE, FSDP = range(5)
GAIN_ROWS = 2 * D // HEAD_COLS + 1


def core_swap(block):
    return lax.ppermute(block, "core", [(0, 1), (1, 0)])


def zz_xor(block, k):
    return lax.ppermute(block, "zz", [(i, i ^ k) for i in range(RINGS)])


def tt_from(block, offset):
    count = lax.axis_size("tt")
    return lax.ppermute(block, "tt", [((i + offset) % count, i) for i in range(count)])


def exchange(blocks, axes):
    return lax.all_to_all(blocks, axes, split_axis=0, concat_axis=0, tiled=True)


def gather_from(copies):
    straight = exchange(copies, ("zz",))
    return [straight, core_swap(straight)]


def cross_send(parts):
    tt_count, fsdp_count = lax.axis_size("tt"), lax.axis_size("fsdp")
    if tt_count != 2 or fsdp_count != 2:
        came = exchange(jnp.stack(parts), ("tt", "fsdp"))
        return [came[n] for n in range(tt_count * fsdp_count)]
    pairs = [[(n, n ^ i) for n in range(4)] for i in range(4)]
    return [parts[0]] + [lax.ppermute(parts[i], ("tt", "fsdp"), pairs[i]) for i in (3, 1, 2)]


SMEM = pl.BlockSpec(memory_space=pltpu.SMEM)
VMEM = pl.BlockSpec(memory_space=pltpu.VMEM)
ANY = pl.BlockSpec(memory_space=pl.ANY)


STATED = 0.1
MXU_FLOPS = 1.15e9


def stated(micros):
    return pl.CostEstimate(
        flops=int(micros * STATED * MXU_FLOPS), bytes_accessed=1, transcendentals=0
    )


def run_kernel(micros, kernel, outs, args, scratch=(), scalars=0, after=(), limit=64):
    skip = len(after)
    return pl.pallas_call(
        lambda *refs: kernel(*refs[skip:]),
        out_shape=tuple(outs),
        in_specs=[ANY] * skip + [SMEM] * scalars + [VMEM] * (len(args) - scalars),
        out_specs=(VMEM,) * len(outs),
        scratch_shapes=list(scratch),
        compiler_params=pltpu.CompilerParams(vmem_limit_bytes=limit * MIB),
        cost_estimate=stated(micros),
    )(*after, *args)


def shape(*dims, dtype=F32):
    return jax.ShapeDtypeStruct(dims, dtype)


def low(*dims):
    return shape(*dims, dtype=BF16)


def at_row(index, rows):
    return pl.ds(pl.multiple_of(index * rows, rows), rows)


def lanes_of(rows):
    return lax.broadcasted_iota(I32, (rows, 2 * HEAD_SIZE), 1)


def swap_halves(values, lanes):
    half = HEAD_SIZE // 2
    return jnp.where(
        lanes % HEAD_SIZE < half,
        pltpu.roll(values, 2 * HEAD_SIZE - half, 1),
        pltpu.roll(values, half, 1),
    )


def widen(cosine, sine):
    return (
        jnp.concatenate([cosine] * 4, axis=1),
        jnp.concatenate([-sine, sine, -sine, sine], axis=1),
    )


def head_sums(values, lanes):
    left = jnp.sum(jnp.where(lanes < HEAD_SIZE, values, 0.0), axis=1, keepdims=True)
    right = jnp.sum(jnp.where(lanes < HEAD_SIZE, 0.0, values), axis=1, keepdims=True)
    return jnp.where(lanes < HEAD_SIZE, left, right)


def to_row(column):
    wide = jnp.broadcast_to(column, (column.shape[0], 2 * HEAD_SIZE))
    return jnp.transpose(wide)[:1]


def to_column(row):
    wide = jnp.broadcast_to(row, (2 * HEAD_SIZE, row.shape[1]))
    return jnp.transpose(wide)[:, :1]


def heads_kernel(attn_ref, heads_ref):
    keys = QUERY_WIDTH
    values = QUERY_WIDTH + KEY_WIDTH
    for h in range(SLOTS):
        heads_ref[h] = jnp.concatenate(
            [
                attn_ref[:, h * PAIR : (h + 1) * PAIR],
                attn_ref[:, keys + h * HEAD_SIZE : keys + (h + 1) * HEAD_SIZE],
                attn_ref[:, values + h * HEAD_SIZE : values + (h + 1) * HEAD_SIZE],
            ],
            axis=1,
        ).astype(BF16)


def units_kernel(ffn_ref, heads_ref, units_ref, in_ref):
    units_ref[...] = ffn_ref[...].astype(BF16)
    part = heads_ref.shape[1]
    per = D // HEAD_COLS
    for h in range(SLOTS):
        in_ref[
            (h // per) * part : (h // per + 1) * part,
            (h % per) * HEAD_COLS : (h % per + 1) * HEAD_COLS,
        ] = heads_ref[h]


def block_kernel(tokens_ref, weights_ref, block_ref):
    rows = tokens_ref.shape[0]
    block_ref[:rows] = tokens_ref[...]
    block_ref[rows:] = weights_ref[:, QUERY_WIDTH + 2 * KEY_WIDTH :].astype(BF16)


def repeat_kernel(heads_ref, copies_ref):
    for n in range(copies_ref.shape[0]):
        copies_ref[n] = heads_ref[...]


def token_kernel(tt_count, run, place_ref, order_ref, lengths_ref, *refs):
    key_row_ref, first_row_ref, position_ref, wide_ref = refs
    chunk = tt_count * 2 * SLOTS * run
    rows = tt_count * 2 * RINGS * run
    tt, core = place_ref[TT], place_ref[CORE]
    offsets = lax.broadcasted_iota(I32, (run, 2 * HEAD_SIZE), 0)
    for b in range(RINGS):
        for v in range(tt_count):
            group = lax.rem(tt + v, tt_count)
            for u in range(tt_count):
                for s in range(2):
                    block = (b * tt_count + lax.rem(group + u, tt_count)) * 2 + (core ^ s)
                    for slot in range(SLOTS):
                        sender = ((slot // 2) * tt_count + group) * 2 + slot % 2
                        start = block * rows + order_ref[block, sender] * run
                        base = v * chunk + ((u * 2 + s) * SLOTS + slot) * run
                        wide_ref[base : base + run] = (offsets + start).astype(F32)
        key_row_ref[b] = jnp.transpose(wide_ref[...])[:1]
        own = wide_ref[:chunk]
        first = jnp.zeros_like(own)
        begin = 0
        for k in range(lengths_ref.shape[0]):
            begin_f = jnp.full_like(own, begin).astype(F32)
            first = jnp.maximum(first, jnp.where(own >= begin_f, begin_f, 0.0))
            begin = begin + lengths_ref[k]
        first_row_ref[b] = jnp.transpose(first)[:1]
        position_ref[b * chunk : (b + 1) * chunk] = own[:, :1] - first[:, :1]


def cotangent_kernel(tt_count, run, place_ref, order_ref, cotangent_ref, mask_ref, *refs):
    own_ref, away_refs, masked_ref, sorted_ref = refs[0], refs[1:-2], refs[-2], refs[-1]
    rows = cotangent_ref.shape[0]
    mask = jnp.transpose(jnp.broadcast_to(mask_ref[...].astype(F32), (rows, rows)))[:, :1]
    masked = jnp.where(mask > 0.0, cotangent_ref[...].astype(F32), 0.0)
    masked_ref[...] = masked.reshape(masked_ref.shape)
    zz, tt, core = place_ref[ZZ], place_ref[TT], place_ref[CORE]
    block = (zz * tt_count + tt) * 2 + core
    for v in range(tt_count):
        group = lax.rem(tt + v, tt_count)
        for slot in range(SLOTS):
            sender = ((slot // 2) * tt_count + group) * 2 + slot % 2
            sorted_ref[slot * run : (slot + 1) * run] = masked_ref[order_ref[block, sender]]
        out_ref = own_ref if v == 0 else away_refs[v - 1]
        out_ref[...] = sorted_ref[...].astype(BF16)


def copies_kernel(*refs):
    part_refs, out_ref = refs[:-1], refs[-1]
    rows = part_refs[0].shape[0]
    for n in range(RINGS):
        for u, ref in enumerate(part_refs):
            out_ref[n, u * rows : (u + 1) * rows] = ref[...]


def project_kernel(tt_count, fsdp_count, run, place_ref, *refs):
    chunk_refs, parts_ref, refs = refs[:SLOTS], refs[SLOTS], refs[SLOTS + 1 :]
    norm_ref, gain_ref, cos_ref, sin_ref = refs[:4]
    inputs_ref, normed_ref, own_ref, query_ref, both_ref, linear_ref, weights_ref = refs[4:11]
    out_part_ref, wide_cos_ref, wide_sin_ref, sorted_ref, part_ref = refs[11:]
    rows = part_ref.shape[0] * run
    piece = SLOTS * run
    slot, zz, tt, core = (place_ref[i] for i in (SLOT, ZZ, TT, CORE))
    part_rows = parts_ref.shape[2]
    for n in range(parts_ref.shape[0]):
        t, f = n // fsdp_count, n % fsdp_count
        for m in range(SLOTS):
            device = (((m // 2) * tt_count + t) * 2 + m % 2) * fsdp_count + f
            weights_ref[device * part_rows : (device + 1) * part_rows] = parts_ref[n, m]
    for n in range(SLOTS):
        part_ref[...] = chunk_refs[n][:rows].astype(F32).reshape(part_ref.shape)
        out_part_ref[slot ^ n] = chunk_refs[n][rows:]
        for b in range(RINGS):
            for u in range(tt_count):
                for s in range(2):
                    block = (b * tt_count + lax.rem(tt + u, tt_count)) * 2 + (core ^ s)
                    base = ((b * tt_count + u) * 2 + s) * SLOTS + (slot ^ n)
                    sorted_ref[base] = part_ref[block]
    for u in range(tt_count):
        own = sorted_ref[pl.ds((zz * tt_count + u) * 2 * SLOTS, SLOTS)]
        own_ref[u * piece : (u + 1) * piece] = own.reshape(piece, D).astype(BF16)
    step = SLOTS * rows // RINGS
    lanes = lanes_of(step)
    key_part = lanes < HEAD_SIZE
    for a in range(RINGS):
        at = slice(a * step, (a + 1) * step)
        values = sorted_ref[a * step // run : (a + 1) * step // run].reshape(step, D)
        inputs_ref[at] = values.astype(BF16)
        normed = (rms_parts(values)[1] * norm_ref[...]).astype(BF16)
        normed_ref[at] = normed
        linear = mm(normed, weights_ref[...], 1, 0)
        linear_ref[at] = linear
        query, both = linear[:, :PAIR], linear[:, PAIR:]
        cosine, sine = widen(cos_ref[at], sin_ref[at])
        wide_cos_ref[at], wide_sin_ref[at] = cosine, sine
        query_factor = lax.rsqrt(head_sums(query * query, lanes) / HEAD_SIZE + EPSILON)
        query = query * query_factor * gain_ref[:, :PAIR]
        query = query * cosine + swap_halves(query, lanes) * sine
        query_ref[at] = query.astype(BF16)
        key_factor = lax.rsqrt(head_sums(both * both, lanes) / HEAD_SIZE + EPSILON)
        key = both * key_factor * gain_ref[:, PAIR:]
        key = key * cosine + swap_halves(key, lanes) * sine
        both_ref[at] = jnp.where(key_part, key, both).astype(BF16)


def spread_keys(both_refs, keys_ref, values_ref, chunk, filler):
    lanes = lanes_of(chunk)
    left = lanes < HEAD_SIZE
    for b in range(RINGS):
        for u, ref in enumerate(both_refs):
            both = ref[b * chunk : (b + 1) * chunk].astype(F32)
            turned = pltpu.roll(both, HEAD_SIZE, 1)
            at = slice(u * chunk, (u + 1) * chunk)
            keys_ref[b, at] = jnp.where(left, both, turned).astype(BF16)
            values_ref[b, 0, at] = jnp.where(left, turned, filler).astype(BF16)
            values_ref[b, 1, at] = jnp.where(left, filler, both).astype(BF16)


def one_head(values, lanes, head):
    keep = lanes < HEAD_SIZE if head == 0 else lanes >= HEAD_SIZE
    return jnp.where(keep, values, jnp.zeros_like(values))


def attend_kernel(tt_count, query_ref, *refs):
    both_refs, refs = refs[:tt_count], refs[tt_count:]
    key_row_ref, first_ref = refs[:2]
    mixed_low_ref, mixed_ref, totals_ref = refs[2:5]
    keys_ref, values_ref, numer_ref = refs[5:]
    chunk = query_ref.shape[0] // RINGS
    spread_keys(both_refs, keys_ref, values_ref, chunk, 1.0)
    lanes = lanes_of(chunk)
    for a in range(RINGS):
        at = slice(a * chunk, (a + 1) * chunk)
        query = query_ref[at]
        queries = [one_head(query, lanes, h) for h in range(GROUP)]
        token, first = to_column(key_row_ref[a, :, :chunk]), to_column(first_ref[a])
        numer_ref[...] = jnp.zeros_like(numer_ref)

        def add(b, visible):
            for h in range(GROUP):
                scores = mm(queries[h], keys_ref[b], 1, 1)
                weight = jnp.where(
                    visible, jnp.exp2(scores * (SCALE * LOG2E) - SHIFT * LOG2E), 0.0
                )
                numer_ref[h] += mm(weight.astype(BF16), values_ref[b, h], 1, 0)

        def below(b, carry):
            add(b, key_row_ref[b] >= first)
            return carry

        lax.fori_loop(0, a, below, 0)
        add(a, (key_row_ref[a] >= first) & (key_row_ref[a] <= token))
        numer = jnp.where(lanes < HEAD_SIZE, numer_ref[0], numer_ref[1])
        totals = pltpu.roll(
            jnp.where(lanes < HEAD_SIZE, numer_ref[1], numer_ref[0]), HEAD_SIZE, 1
        )
        mixed = numer / totals
        mixed_ref[at] = mixed
        mixed_low_ref[at] = mixed.astype(BF16)
        totals_ref[at] = totals


def turn(values):
    return jnp.transpose(values.astype(F32)).astype(BF16)


def out_weights_kernel(
    tt_count, fsdp_count, parts_ref, units_ref, passed_ref, out_ref, out_turned_ref, turned_ref, copy_ref
):
    rows = parts_ref.shape[2]
    for t in range(tt_count):
        for f in range(fsdp_count):
            for m in range(SLOTS):
                device = (((m // 2) * tt_count + t) * 2 + m % 2) * fsdp_count + f
                out_ref[device * rows : (device + 1) * rows] = parts_ref[t * fsdp_count + f, m]
    copy_ref[...] = passed_ref[...]
    step = 2 * PAIR
    for n in range(0, D, step):
        out_turned_ref[n : n + step] = turn(out_ref[:, n : n + step])
        for i in range(3):
            turned_ref[i, n : n + step] = turn(units_ref[:, i * D + n : i * D + n + step])


def in_weights_kernel(cross, parts_ref, out_ref):
    half = parts_ref.shape[2] // 2
    for n in range(2 * cross):
        for z in range(RINGS):
            device = z * 2 * cross + n
            at = slice(device * half, (device + 1) * half)
            out_ref[at, :D] = parts_ref[n, z, :half]
            out_ref[at, D:] = parts_ref[n, z, half:]


def feed_kernel(tt_count, skip, place_ref, *refs):
    refs = refs[skip:]
    mixed_refs, inputs_ref, cot_refs = refs[:2], refs[2], refs[3:5]
    out_turned_hbm, turned_hbm, units_hbm, norm_ref = refs[5:9]
    refs = refs[9:]
    hidden_ref, normed_ref, active_ref, gate_ref, up_ref, grad_ref = refs[:6]
    mid_own_ref, out_own_ref, out_away_ref, mid_away_refs = refs[6], refs[7], refs[8], refs[9:11]
    all_ref, out_turned_ref, turned_ref, units_ref = refs[11:15]
    hidden_all_ref, mid_ref, out_ref, sems = refs[15:]
    step = pl.program_id(0)
    copies = [
        pltpu.make_async_copy(out_turned_hbm, out_turned_ref, sems.at[0]),
        pltpu.make_async_copy(turned_hbm, turned_ref, sems.at[1]),
        pltpu.make_async_copy(units_hbm, units_ref, sems.at[2]),
    ]

    @pl.when(step == 0)
    def _():
        for copy in copies:
            copy.start()

    rows = cot_refs[0].shape[1]
    piece = rows // tt_count
    core = place_ref[CORE]
    for c in range(2):
        for z in range(RINGS):
            column = pl.ds(pl.multiple_of((z * 2 + (core ^ c)) * PAIR, PAIR), PAIR)
            for u in range(tt_count):
                for s in range(2):
                    to = (u * 2 + s) * piece
                    source = (u * 2 + (s ^ c)) * piece
                    all_ref[to : to + piece, column] = mixed_refs[c][z, source : source + piece]
    for u in range(tt_count):
        for s in range(2):
            to = (u * 2 + s) * piece
            grad_ref[0, to : to + piece] = cot_refs[s][0, u * piece : (u + 1) * piece]

    @pl.when(step == 0)
    def _():
        copies[0].wait()

    hidden = inputs_ref[...].astype(F32) + mm(all_ref[...], out_turned_ref[...], 1, 0)
    hidden_all_ref[...] = hidden
    normed = (rms_parts(hidden)[1] * norm_ref[...]).astype(BF16)
    normed_ref[0] = normed

    @pl.when(step == 0)
    def _():
        copies[1].wait()

    gate = mm(normed, turned_ref[0], 1, 0)
    up = mm(normed, turned_ref[1], 1, 0)
    sigmoid = 1.0 / (1.0 + jnp.exp(-gate))
    swish = gate * sigmoid
    active = (swish * up).astype(BF16)
    grad_act = mm(grad_ref[0], turned_ref[2], 1, 0)
    grad_up = (grad_act * swish).astype(BF16)
    grad_gate = (grad_act * up * sigmoid * (1.0 + gate * (1.0 - sigmoid))).astype(BF16)
    active_ref[0] = active
    gate_ref[0] = grad_gate
    up_ref[0] = grad_up

    @pl.when(step == 0)
    def _():
        copies[2].wait()

    mid_ref[...] = mm(grad_gate, units_ref[:, :D], 1, 0) + mm(
        grad_up, units_ref[:, D : 2 * D], 1, 0
    )
    out_ref[...] = mm(active, units_ref[:, 2 * D :], 1, 0)
    for u in range(tt_count):
        to = slice(u * piece, (u + 1) * piece)
        own = slice(2 * u * piece, (2 * u + 1) * piece)
        away = slice((2 * u + 1) * piece, (2 * u + 2) * piece)
        hidden_ref[to] = hidden_all_ref[own]
        mid_own_ref[0, to] = mid_ref[own]
        out_own_ref[0, to] = out_ref[own]
        out_away_ref[0, to] = out_ref[away].astype(BF16)
    for i, ref in enumerate(mid_away_refs):

        @pl.when(step == i)
        def _():
            for u in range(tt_count):
                away = slice((2 * u + 1) * piece, (2 * u + 2) * piece)
                ref[u * piece : (u + 1) * piece] = mid_ref[away].astype(BF16)


def feed(
    first_k, steps, after, tt_count, place, mixed, inputs, cot, out_turned, turned, units, norm_mid
):
    rows = cot[0].shape[1]
    unit_count = units.shape[0]

    def quarter(i, place):
        return place[ZZ] ^ (first_k - i)

    def a_step(outs):
        return [pl.BlockSpec((1,) + o.shape[1:], lambda i, place: (i, 0, 0)) for o in outs]

    def whole(array):
        return pl.BlockSpec(array.shape, lambda i, place: (0, 0))

    hidden = shape(rows, D)
    outs = [
        low(steps, 2 * rows, D),
        low(steps, 2 * rows, unit_count),
        low(steps, 2 * rows, unit_count),
        low(steps, 2 * rows, unit_count),
        low(steps, 2 * rows, D),
        shape(steps, rows, D),
        shape(steps, rows, D),
        low(steps, rows, D),
    ]
    away = [low(rows, D)] * steps
    return pl.pallas_call(
        functools.partial(feed_kernel, tt_count, len(after)),
        out_shape=tuple([hidden] + outs + away),
        grid_spec=pltpu.PrefetchScalarGridSpec(
            num_scalar_prefetch=1,
            grid=(steps,),
            in_specs=[ANY] * len(after)
            + [
                pl.BlockSpec((RINGS, 2 * rows, PAIR), lambda i, p: (0, quarter(i, p), 0)),
                pl.BlockSpec((RINGS, 2 * rows, PAIR), lambda i, p: (0, quarter(i, p), 0)),
                pl.BlockSpec((2 * rows, D), lambda i, p: (quarter(i, p), 0)),
                pl.BlockSpec((1, rows, D), lambda i, p: (quarter(i, p), 0, 0)),
                pl.BlockSpec((1, rows, D), lambda i, p: (quarter(i, p), 0, 0)),
                ANY,
                ANY,
                ANY,
                whole(norm_mid),
            ],
            out_specs=tuple([whole(hidden)] + a_step(outs) + [whole(a) for a in away]),
            scratch_shapes=[
                pltpu.VMEM((2 * rows, QUERY_WIDTH), BF16),
                pltpu.VMEM(out_turned.shape, BF16),
                pltpu.VMEM(turned.shape, BF16),
                pltpu.VMEM(units.shape, BF16),
                pltpu.VMEM((2 * rows, D), F32),
                pltpu.VMEM((2 * rows, D), F32),
                pltpu.VMEM((2 * rows, D), F32),
                pltpu.SemaphoreType.DMA((3,)),
            ],
        ),
        compiler_params=pltpu.CompilerParams(vmem_limit_bytes=64 * MIB),
        cost_estimate=stated(14),
    )(place, *after, *mixed, inputs, *cot, out_turned, turned, units, norm_mid)


def far_kernel(own_ref, swapped_far_ref, swapped_next_ref, passed_ref, sum_ref, copy_ref):
    for n, ref in enumerate((swapped_far_ref, swapped_next_ref)):
        sum_ref[n] = (own_ref[n] + ref[...].astype(F32)).astype(BF16)
    copy_ref[...] = passed_ref[...]


def next_kernel(own_ref, swapped_ref, far_ref, sum_ref):
    total = own_ref[0] + swapped_ref[...].astype(F32) + far_ref[0].astype(F32)
    sum_ref[...] = total.astype(BF16)


def middle_kernel(tt_count, *refs):
    own_ref, swapped_ref, far_ref, next_ref, refs = *refs[:4], refs[4:]
    hidden_ref, cot_ref, out_weights_ref, norm_ref = refs[:4]
    inputs_ref, refs = refs[4], refs[5:]
    send_ref, gain_ref, pack_refs = refs[0], refs[1], refs[2:]
    grad_mid = own_ref[1] + swapped_ref[...].astype(F32)
    grad_mid += far_ref[1].astype(F32) + next_ref[...].astype(F32)
    factor, unit = rms_parts(hidden_ref[...])
    gain_ref[...] = jnp.sum(grad_mid * unit, axis=0, keepdims=True)
    grad_hidden = cot_ref[...].astype(F32) + norm_back(grad_mid * norm_ref[...], unit, factor)
    hidden_low = grad_hidden.astype(BF16)
    piece = pack_refs[0].shape[1]
    for u, ref in enumerate(pack_refs):
        at = slice(u * piece, (u + 1) * piece)
        ref[0] = inputs_ref[at]
        ref[1] = hidden_low[at]
    grad_mixed = mm(hidden_low, out_weights_ref[...], 1, 0).astype(BF16)
    width = (send_ref.shape[2] - PAIR) // tt_count
    for n in range(SLOTS):
        send_ref[n, :, :PAIR] = grad_mixed[:, n * PAIR : (n + 1) * PAIR]
        parts = []
        for t in range(tt_count):
            base = (((n // 2) * tt_count + t) * 2 + n % 2) * width
            parts.append(grad_hidden[:, base : base + width])
        send_ref[n, :, PAIR:] = jnp.concatenate(parts, axis=1).astype(BF16)


def out_sum_kernel(place_ref, own_far, own_near, swapped_far, swapped_near, send_ref, here_ref):
    zz = place_ref[ZZ]
    for k in range(RINGS):
        own, swapped = (own_far, swapped_far) if k > 1 else (own_near, swapped_near)
        total = own[1 - k % 2] + swapped[1 - k % 2].astype(F32)
        send_ref[zz ^ k] = total.astype(BF16)
        if k == 0:
            here_ref[...] = total


def result_kernel(place_ref, hidden_ref, own_ref, arrived_ref, *pack_refs):
    zz = place_ref[ZZ]
    result = hidden_ref[...] + own_ref[...]
    for k in range(1, RINGS):
        result += arrived_ref[zz ^ k].astype(F32)
    result = result.astype(BF16)
    piece = pack_refs[0].shape[0]
    for u, ref in enumerate(pack_refs):
        ref[...] = result[u * piece : (u + 1) * piece]


def attend_back_kernel(tt_count, place_ref, query_ref, *refs):
    both_refs, refs = refs[:tt_count], refs[tt_count:]
    grad_mixed_ref, mixed_ref, totals_ref = refs[:3]
    key_row_ref, first_ref = refs[3:5]
    grad_query_ref, grad_own_ref, refs = refs[5], refs[6], refs[7:]
    grad_away_refs, refs = refs[: tt_count - 1], refs[tt_count - 1 :]
    keys_ref, values_ref, turned_ref, grad_both_ref, sorted_ref, query_sum_ref, column_ref = refs
    total = query_ref.shape[0]
    chunk = total // RINGS
    piece = total // SLOTS // tt_count
    spread_keys(both_refs, keys_ref, values_ref, chunk, -1.0)
    key_count = tt_count * chunk
    for b in range(RINGS):
        turned_ref[b] = jnp.transpose(keys_ref[b].astype(F32)[:, :HEAD_SIZE]).astype(BF16)
        column_ref[b] = to_column(key_row_ref[b])
    grad_both_ref[...] = jnp.zeros_like(grad_both_ref)
    core = place_ref[CORE]
    for n in range(SLOTS):
        for u in range(tt_count):
            to = ((n // 2) * tt_count + u) * 2 + (core ^ (n % 2))
            sorted_ref[at_row(to, piece)] = grad_mixed_ref[
                n, u * piece : (u + 1) * piece, :PAIR
            ].astype(F32)
    lanes = lanes_of(chunk)
    left = lanes < HEAD_SIZE
    for a in range(RINGS):
        at = slice(a * chunk, (a + 1) * chunk)
        query = query_ref[at]
        grad_mixed, totals = sorted_ref[at], totals_ref[at]
        grad_numer = (grad_mixed / totals).astype(BF16).astype(F32)
        delta = head_sums(grad_mixed * mixed_ref[at], lanes) / totals
        high = delta.astype(BF16).astype(F32)
        middle = (delta - high).astype(BF16).astype(F32)
        parts = jnp.where(
            lanes % HEAD_SIZE == 0,
            high,
            jnp.where(
                lanes % HEAD_SIZE == 1,
                middle,
                jnp.where(lanes % HEAD_SIZE == 2, delta - high - middle, 0.0),
            ),
        )
        parts = pltpu.roll(parts, HEAD_SIZE, 1)
        query_f = query.astype(F32)
        query_turned = pltpu.roll(query_f, HEAD_SIZE, 1)
        numer_turned = pltpu.roll(grad_numer, HEAD_SIZE, 1)
        queries = [one_head(query, lanes, h) for h in range(GROUP)]
        grads = [
            jnp.where(left, grad_numer, parts).astype(BF16),
            jnp.where(left, parts, grad_numer).astype(BF16),
        ]
        query_left = [
            jnp.where(left, query_f, 0.0).astype(BF16),
            jnp.where(left, query_turned, 0.0).astype(BF16),
        ]
        numer_right = [
            jnp.where(left, 0.0, numer_turned).astype(BF16),
            jnp.where(left, 0.0, grad_numer).astype(BF16),
        ]
        token, first = key_row_ref[a][:, :chunk], first_ref[a]
        query_sum_ref[...] = jnp.zeros_like(query_sum_ref)

        def add(b, visible):
            added = jnp.zeros((key_count, 2 * HEAD_SIZE), F32)
            for h in range(GROUP):
                scores = mm(keys_ref[b], queries[h], 1, 1)
                weight = jnp.where(
                    visible, jnp.exp2(scores * (SCALE * LOG2E) - SHIFT * LOG2E), 0.0
                )
                grad_weight = mm(values_ref[b, h], grads[h], 1, 1)
                grad_score = (weight * grad_weight).astype(BF16)
                added += mm(grad_score, query_left[h], 1, 0)
                added += mm(weight.astype(BF16), numer_right[h], 1, 0)
                query_sum_ref[h] += mm(turned_ref[b], grad_score, 1, 0)
            grad_both_ref[b] += added

        def below(b, carry):
            add(b, column_ref[b] >= first)
            return carry

        lax.fori_loop(0, a, below, 0)
        add(a, (column_ref[a] >= first) & (column_ref[a] <= token))
        grad_query_ref[at] = SCALE * jnp.transpose(
            jnp.concatenate([query_sum_ref[0], query_sum_ref[1]], axis=0)
        )
    for b in range(RINGS):
        at = slice(b * chunk, (b + 1) * chunk)
        for u in range(tt_count):
            part = grad_both_ref[b, u * chunk : (u + 1) * chunk]
            part = jnp.where(left, part * SCALE, part)
            if u == 0:
                grad_own_ref[at] = part
            else:
                grad_away_refs[u - 1][at] = part.astype(BF16)


def project_back_kernel(tt_count, place_ref, linear_ref, grad_query_ref, grad_own_ref, *refs):
    arrived_refs, refs = refs[: tt_count - 1], refs[tt_count - 1 :]
    gain_ref, cos_ref, sin_ref, proj_ref, grad_ref, gains_ref = refs
    total = grad_query_ref.shape[0]
    step = total // RINGS
    piece = step // tt_count // 2
    lanes = lanes_of(step)
    key_part = lanes < HEAD_SIZE
    tt, core = place_ref[TT], place_ref[CORE]
    sums = jnp.zeros((1, HEAD_COLS), F32)
    for a in range(RINGS):
        at = slice(a * step, (a + 1) * step)
        linear = linear_ref[at]
        cosine, sine = cos_ref[at], sin_ref[at]
        grad_both = grad_own_ref[at]
        for ref in arrived_refs:
            grad_both += ref[at].astype(F32)
        parts, gains = [], []
        for grad, values, gain in (
            (grad_query_ref[at], linear[:, :PAIR], gain_ref[:, :PAIR]),
            (grad_both, linear[:, PAIR:], gain_ref[:, PAIR:]),
        ):
            factor = lax.rsqrt(head_sums(values * values, lanes) / HEAD_SIZE + EPSILON)
            unit = values * factor
            grad_norm = grad * cosine - swap_halves(grad, lanes) * sine
            gains.append(jnp.sum(grad_norm * unit, axis=0, keepdims=True))
            hat = grad_norm * gain
            mean = head_sums(hat * unit, lanes) / HEAD_SIZE
            parts.append(factor * (hat - unit * mean))
        parts[1] = jnp.where(key_part, parts[1], grad_both)
        grad_low = jnp.concatenate(parts, axis=1).astype(BF16)
        grad_ref[at] = grad_low
        for u in range(tt_count):
            for s in range(2):
                block = (a * tt_count + lax.rem(tt + u, tt_count)) * 2 + (core ^ s)
                base = (u * 2 + s) * piece
                proj_ref[block] = grad_low[base : base + piece]
        sums += jnp.concatenate(gains, axis=1)
    gains_ref[...] = sums


def head_grad_kernel(tt_count, fsdp_count, relative, place_ref, *refs):
    normed_ref, grad_ref, weights_ref, norm_ref, mid_ref, head_ref, out_grad_ref = refs[:7]
    out_refs, product_ref = refs[7:-1], refs[-1]
    rows = out_grad_ref.shape[0] // tt_count // fsdp_count
    half = rows // 2
    tt, fsdp = place_ref[TT], place_ref[FSDP]
    product_ref[...] = mm(normed_ref[...], grad_ref[...], 0, 0)
    column = jnp.sum(product_ref[...] * weights_ref[...].astype(F32), axis=1, keepdims=True)
    gain_in = to_row(column) / norm_ref[...]
    parts = [
        row[:, i : i + HEAD_COLS]
        for row in (gain_in, mid_ref[...], head_ref[...])
        for i in range(0, row.shape[1], HEAD_COLS)
    ]
    gains = jnp.concatenate(parts, axis=0)
    for n, out_ref in enumerate(out_refs):
        t, f = n // fsdp_count, n % fsdp_count
        if relative:
            t, f = t ^ tt, f ^ fsdp
        for m in range(SLOTS):
            device = (((m // 2) * tt_count + t) * 2 + m % 2) * fsdp_count + f
            part = product_ref[at_row(device, rows)]
            out = out_grad_ref[
                at_row(t * fsdp_count + f, rows), (m % 4) * HEAD_COLS : (m % 4 + 1) * HEAD_COLS
            ][(m // 4) * half : (m // 4 + 1) * half]
            out_ref[m] = jnp.concatenate([part, out, gains], axis=0).astype(BF16)


def sum_kernel(*refs):
    part_refs, tail_ref, out_ref = refs[:-2], refs[-2], refs[-1]
    rows = out_ref.shape[0]
    half = rows // 2
    for m in range(SLOTS):
        total = part_refs[0][m].astype(F32)
        for ref in part_refs[1:]:
            total += ref[m].astype(F32)
        tail_ref[m] = jnp.concatenate([total[:rows], total[rows + half :]], axis=0).astype(BF16)
        out_ref[
            (m // 4) * half : (m // 4 + 1) * half, (m % 4) * HEAD_COLS : (m % 4 + 1) * HEAD_COLS
        ] = total[rows : rows + half]


def out_grad_kernel(tt_count, place_ref, *refs):
    mixed_refs, columns_ref, product_ref, turned_ref = refs[:2], refs[2], refs[3], refs[4]
    total = mixed_refs[0].shape[1]
    piece = total // SLOTS // tt_count
    core = place_ref[CORE]
    for n in range(SLOTS):
        for u in range(tt_count):
            part = columns_ref[n, u * piece : (u + 1) * piece, PAIR:]
            for c in range(2):
                to = ((n // 2) * tt_count + u) * 2 + (core ^ c ^ (n % 2))
                turned_ref[c, at_row(to, piece)] = part
    for c in range(2):
        turned = jnp.transpose(turned_ref[c].astype(F32)).astype(BF16)
        for z in range(RINGS):
            column = pl.ds(pl.multiple_of((z * 2 + (core ^ c)) * PAIR, PAIR), PAIR)
            product_ref[:, column] = mm(turned, mixed_refs[c][z], 1, 0)


def unit_grad_kernel(*refs):
    fed, out_ref = (refs[:5], refs[5:10]), refs[10]
    rows_ref, product_ref, normed_ref, grad_ref = refs[-4:]
    step = fed[0][0].shape[1]

    def collect(index, to_ref):
        at = 0
        for call in fed:
            for i in range(call[index].shape[0]):
                to_ref[at : at + step] = call[index][i]
                at += step

    collect(0, normed_ref)
    collect(4, grad_ref)
    for index, other_ref, column in ((2, normed_ref, 0), (3, normed_ref, D), (1, grad_ref, 2 * D)):
        collect(index, rows_ref)
        product_ref[...] = mm(rows_ref[...], other_ref[...], 0, 0)
        out_ref[:, column : column + D] = product_ref[...].astype(BF16)


def unit_adam_kernel(*refs):
    grad_refs, refs = refs[:-7], refs[-7:]
    weight_ref, first_ref, second_ref, rate_ref, grad_ref, second_new_ref, new_ref = refs
    grad = grad_refs[0][...].astype(F32)
    for ref in grad_refs[1:]:
        grad += ref[...].astype(F32)
    grad_ref[...] = grad
    new, second_new = adam_update(
        weight_ref[...], grad, first_ref[...], second_ref[...], rate_ref[...]
    )
    new_ref[...] = new
    second_new_ref[...] = second_new


def attn_adam_kernel(tail_ref, out_ref, *refs):
    weight_ref, first_ref, second_ref, rate_ref = refs[:4]
    gains_ref, gain_first_ref, gain_second_ref = refs[4:7]
    grad_ref, second_new_ref, new_ref = refs[7:10]
    gain_grad_ref, gain_second_new_ref, gain_new_ref = refs[10:]
    rows = weight_ref.shape[0]
    queries, keys, values = [], [], []
    gains = jnp.zeros((GAIN_ROWS, HEAD_COLS), F32)
    for n in range(SLOTS):
        part = tail_ref[n].astype(F32)
        gains += part[rows:]
        queries.append(part[:rows, :PAIR])
        keys.append(part[:rows, PAIR : PAIR + HEAD_SIZE])
        values.append(part[:rows, PAIR + HEAD_SIZE :])
    grad = jnp.concatenate(queries + keys + values + [out_ref[...]], axis=1)
    grad_ref[...] = grad
    new, second_new = adam_update(
        weight_ref[...], grad, first_ref[...], second_ref[...], rate_ref[...]
    )
    new_ref[...] = new
    second_new_ref[...] = second_new
    lanes = gains_ref.shape[1]
    per = 2 * D // HEAD_COLS
    lines = [
        gains[i : i + 1, j : j + lanes] for i in range(per) for j in range(0, HEAD_COLS, lanes)
    ]
    heads = gains[per : per + 1]
    query = heads[:, :HEAD_SIZE] + heads[:, HEAD_SIZE:PAIR]
    lines.append(jnp.concatenate([query, heads[:, PAIR : PAIR + HEAD_SIZE]], axis=1))
    gain_grad = jnp.concatenate(lines, axis=0)
    gain_grad_ref[...] = gain_grad
    new, second_new = adam_update(
        gains_ref[...], gain_grad, gain_first_ref[...], gain_second_ref[...], GAIN_RATE
    )
    gain_new_ref[...] = new
    gain_second_new_ref[...] = second_new


def last_kernel(tt_count, run, place_ref, order_ref, proj_ref, weights_ref, norm_ref, *refs):
    pack_refs, result_refs, refs = refs[:tt_count], refs[tt_count : 2 * tt_count], refs[2 * tt_count :]
    output_ref, grad_ref, left_ref, inputs_ref, hidden_ref = refs
    piece = SLOTS * run
    zz, tt, core = place_ref[ZZ], place_ref[TT], place_ref[CORE]
    for v in range(tt_count):
        at = slice(v * piece, (v + 1) * piece)
        group = lax.rem(tt + v, tt_count)
        for h in range(SLOTS):
            source = ((h // 2) * tt_count + group) * 2 + h % 2
            left_ref[at, h * HEAD_COLS : (h + 1) * HEAD_COLS] = proj_ref[source]
        inputs_ref[at] = pack_refs[v][0].astype(F32)
        hidden_ref[at] = pack_refs[v][1].astype(F32)
    grad_normed = mm(left_ref[...], weights_ref[...], 1, 1)
    factor, unit = rms_parts(inputs_ref[...])
    back = hidden_ref[...] + norm_back(grad_normed * norm_ref[...], unit, factor)
    block = (zz * tt_count + tt) * 2 + core
    for v in range(tt_count):
        group = lax.rem(tt + v, tt_count)
        result = result_refs[v][...].astype(F32)
        for slot in range(SLOTS):
            sender = ((slot // 2) * tt_count + group) * 2 + slot % 2
            to = order_ref[block, sender]
            base = (v * SLOTS + slot) * run
            output_ref[to] = result[slot * run : (slot + 1) * run]
            grad_ref[to] = back[base : base + run]


def on_device(
    inputs,
    cotangent,
    lengths,
    order,
    pad_mask,
    attn_weights,
    attn_first,
    attn_second,
    ffn_weights,
    ffn_first,
    ffn_second,
    gains,
    gain_first,
    gain_second,
):
    zz, tt, core = lax.axis_index("zz"), lax.axis_index("tt"), lax.axis_index("core")
    fsdp = lax.axis_index("fsdp")
    tt_count, fsdp_count = lax.axis_size("tt"), lax.axis_size("fsdp")
    ctx_count = SLOTS * tt_count
    device_count = ctx_count * fsdp_count
    cross = tt_count * fsdp_count
    square = tt_count == 2 and fsdp_count == 2
    rows = inputs.shape[1]
    run = rows // ctx_count
    piece = SLOTS * run
    group_rows = SLOTS * rows
    chunk = group_rows // RINGS
    key_count = tt_count * chunk
    attn_rows, ffn_rows_own = attn_weights.shape[0], ffn_weights.shape[0]
    unit_count = ffn_rows_own * cross
    place = jnp.stack([zz * 2 + core, zz, tt, core, fsdp]).astype(I32)
    order_table, length_row = order[0], lengths[0]

    norm_in, norm_mid = gains[None, :D], gains[None, D : 2 * D]
    query_gain = gains[2 * D : 2 * D + HEAD_SIZE]
    key_gain = gains[2 * D + HEAD_SIZE :]
    head_gains = jnp.concatenate([query_gain] * GROUP + [key_gain, jnp.ones_like(key_gain)])[None]

    def over_tt(parts):
        return [parts[0]] + [tt_from(parts[tt_count - u], u) for u in range(1, tt_count)]

    (block_own,) = run_kernel(
        1, block_kernel, [low(rows + attn_rows, D)], [inputs[0], attn_weights]
    )
    (heads_low,) = run_kernel(
        1,
        heads_kernel,
        [low(SLOTS, attn_rows, HEAD_COLS)],
        [attn_weights],
        after=[block_own],
    )
    head_own = exchange(heads_low, ("zz", "core"))
    units_own, in_low = run_kernel(
        2,
        units_kernel,
        [low(ffn_rows_own, 3 * D), low(2 * attn_rows, D)],
        [ffn_weights, heads_low],
    )
    cot = run_kernel(
        1.8,
        functools.partial(cotangent_kernel, tt_count, run),
        [low(piece, D)] * tt_count,
        [place, order_table, cotangent[0], pad_mask],
        scratch=[pltpu.VMEM((ctx_count, run, D), F32), pltpu.VMEM((piece, D), F32)],
        scalars=2,
        after=[units_own],
    )
    (head_copies,) = run_kernel(
        0, repeat_kernel, [low(cross, SLOTS, attn_rows, HEAD_COLS)], [head_own]
    )
    straight = [block_own] + [zz_xor(block_own, k) for k in range(1, RINGS)]
    input_parts = [b for part in straight for b in (part, core_swap(part))]
    head_parts = exchange(head_copies, ("tt", "fsdp"))
    key_row, first_row, position = run_kernel(
        2.3,
        functools.partial(token_kernel, tt_count, run),
        [shape(RINGS, 1, key_count), shape(RINGS, 1, chunk), shape(group_rows, 1)],
        [place, order_table, length_row],
        scratch=[pltpu.VMEM((key_count, 2 * HEAD_SIZE), F32)],
        scalars=3,
        after=[cot[0]],
    )

    units = lax.all_gather(units_own, ("tt", "fsdp"), axis=0, tiled=True)
    frequency = jnp.exp(
        jnp.arange(HEAD_SIZE // 2, dtype=F32) * (-2.0 * math.log(ROPE_BASE) / HEAD_SIZE)
    )
    angles = position * frequency[None, :]
    cosine, sine = jnp.cos(angles), jnp.sin(angles)

    (cot_copies,) = run_kernel(
        2,
        copies_kernel,
        [low(RINGS, rows, D)],
        over_tt(cot),
        after=[key_row, cosine, sine] + [straight[k] for k in range(1, RINGS)],
    )
    cot_straight = exchange(cot_copies, ("zz",))
    inputs_sorted, normed, inputs_own, query, both, linear, head_weights, out_part, *table = run_kernel(
        50,
        functools.partial(project_kernel, tt_count, fsdp_count, run),
        [
            low(group_rows, D),
            low(group_rows, D),
            low(rows, D),
            low(group_rows, PAIR),
            low(group_rows, 2 * HEAD_SIZE),
            shape(group_rows, HEAD_COLS),
            low(D, HEAD_COLS),
            low(SLOTS, attn_rows, QUERY_WIDTH),
            shape(group_rows, PAIR),
            shape(group_rows, PAIR),
        ],
        [place] + input_parts + [head_parts, norm_in, head_gains, cosine, sine],
        scratch=[
            pltpu.VMEM((group_rows // run, run, D), F32),
            pltpu.VMEM((ctx_count, run, D), F32),
        ],
        scalars=1,
        after=[cot_copies],
    )
    both_sets = [both] + [tt_from(both, u) for u in range(1, tt_count)]
    out_parts = lax.all_gather(out_part, ("tt", "fsdp"), axis=0)

    key_scratch = pltpu.VMEM((RINGS, key_count, 2 * HEAD_SIZE), BF16)
    value_scratch = pltpu.VMEM((RINGS, GROUP, key_count, 2 * HEAD_SIZE), BF16)
    mixed_low, mixed, totals = run_kernel(
        0,
        functools.partial(attend_kernel, tt_count),
        [low(group_rows, PAIR), shape(group_rows, PAIR), shape(group_rows, PAIR)],
        [query] + both_sets + [key_row, first_row],
        scratch=[
            key_scratch,
            value_scratch,
            pltpu.VMEM((GROUP, chunk, PAIR), F32),
        ],
    )
    (mixed_copies,) = run_kernel(
        0,
        copies_kernel,
        [low(RINGS, group_rows, PAIR)],
        [mixed_low],
        after=[cot_straight, units],
    )
    mixed_parts = gather_from(mixed_copies)
    out_weights, out_turned, units_turned, cot_straight = run_kernel(
        2,
        functools.partial(out_weights_kernel, tt_count, fsdp_count),
        [
            low(D, QUERY_WIDTH),
            low(QUERY_WIDTH, D),
            low(3, D, unit_count),
            low(RINGS, rows, D),
        ],
        [out_parts, units, cot_straight],
        after=[mixed_copies],
    )
    cot_parts = [cot_straight, core_swap(cot_straight)]
    (in_copies,) = run_kernel(
        0, copies_kernel, [low(RINGS, 2 * attn_rows, D)], [in_low], after=[mixed_parts[0]]
    )
    in_straight = exchange(in_copies, ("zz",))

    def feed_half(first_k, after):
        return feed(
            first_k,
            2,
            after,
            tt_count,
            place,
            mixed_parts,
            inputs_sorted,
            cot_parts,
            out_turned,
            units_turned,
            units,
            norm_mid,
        )

    far = feed_half(3, [in_copies])
    far_sums, in_straight = run_kernel(
        0,
        far_kernel,
        [low(2, rows, D), low(*in_straight.shape)],
        [far[6], core_swap(far[9]), core_swap(far[10]), in_straight],
    )
    far_arrived = zz_xor(far_sums, 2)
    in_parts = lax.all_gather(in_straight, ("tt", "core", "fsdp"), axis=0)
    near = feed_half(1, [far_sums])
    swapped = [core_swap(near[9]), core_swap(near[10])]
    (unit_grad,) = run_kernel(
        0,
        unit_grad_kernel,
        [low(unit_count, 3 * D)],
        [half[i] for half in (far, near) for i in (1, 2, 3, 4, 5)],
        scratch=[
            pltpu.VMEM((group_rows, unit_count), BF16),
            pltpu.VMEM((unit_count, D), F32),
            pltpu.VMEM((group_rows, D), BF16),
            pltpu.VMEM((group_rows, D), BF16),
        ],
    )
    unit_sum = lax.psum_scatter(unit_grad, ("tt", "fsdp"), scatter_dimension=0, tiled=True)

    (next_sum,) = run_kernel(
        0,
        next_kernel,
        [low(rows, D)],
        [near[6], swapped[0], far_arrived],
        after=[unit_grad],
    )
    next_arrived = zz_xor(next_sum, 1)
    hidden_own = near[0]
    cot_own = cot_copies[0]
    mixed_send, gain_mid, *packs = run_kernel(
        4,
        functools.partial(middle_kernel, tt_count),
        [low(SLOTS, rows, PAIR + cross * attn_rows), shape(1, D)] + [low(2, piece, D)] * tt_count,
        [near[6], swapped[1], far_arrived, next_arrived]
        + [hidden_own, cot_own, out_weights, norm_mid, inputs_own],
    )
    mixed_here = exchange(mixed_send, ("zz", "core"))
    packs_here = over_tt(packs)

    (in_weights,) = run_kernel(
        0,
        functools.partial(in_weights_kernel, cross),
        [low(D, SLOTS * HEAD_COLS)],
        [in_parts],
        after=[mixed_send],
    )
    out_send, out_own = run_kernel(
        0,
        out_sum_kernel,
        [low(RINGS, rows, D), shape(rows, D)],
        [place, far[7], near[7], core_swap(far[8]), core_swap(near[8])],
        scalars=1,
        after=[in_weights],
    )
    out_arrived = exchange(out_send, ("zz",))

    back = run_kernel(
        1000,
        functools.partial(attend_back_kernel, tt_count),
        [shape(group_rows, PAIR), shape(group_rows, 2 * HEAD_SIZE)]
        + [low(group_rows, 2 * HEAD_SIZE)] * (tt_count - 1),
        [place, query] + both_sets + [mixed_here, mixed, totals, key_row, first_row],
        scratch=[
            key_scratch,
            value_scratch,
            pltpu.VMEM((RINGS, HEAD_SIZE, key_count), BF16),
            pltpu.VMEM((RINGS, key_count, 2 * HEAD_SIZE), F32),
            pltpu.VMEM((group_rows, PAIR), F32),
            pltpu.VMEM((GROUP, HEAD_SIZE, chunk), F32),
            pltpu.VMEM((RINGS, key_count, 1), F32),
        ],
        scalars=1,
        after=[out_send] + packs_here[1:],
    )
    arrived_both = over_tt(back[1:])[1:]
    (out_grad,) = run_kernel(
        3.3,
        functools.partial(out_grad_kernel, tt_count),
        [shape(cross * attn_rows, QUERY_WIDTH)],
        [place] + mixed_parts + [mixed_here],
        scratch=[pltpu.VMEM((2, group_rows, cross * attn_rows), BF16)],
        scalars=1,
        after=[back[0]],
    )
    proj, grad_proj, head_gain = run_kernel(
        5,
        functools.partial(project_back_kernel, tt_count),
        [low(ctx_count, piece, HEAD_COLS), low(group_rows, HEAD_COLS), shape(1, HEAD_COLS)],
        [place, linear, back[0], back[1]] + arrived_both + [head_gains] + table,
        scalars=1,
        after=[out_grad],
    )
    tails = run_kernel(
        4,
        functools.partial(head_grad_kernel, tt_count, fsdp_count, square),
        [low(SLOTS, attn_rows + attn_rows // 2 + GAIN_ROWS, HEAD_COLS)] * cross,
        [place, normed, grad_proj, head_weights, norm_in, gain_mid, head_gain, out_grad],
        scratch=[pltpu.VMEM((D, HEAD_COLS), F32)],
        scalars=1,
    )
    proj_here = exchange(proj, CTX)
    results = run_kernel(
        2.6,
        result_kernel,
        [low(piece, D)] * tt_count,
        [place, hidden_own, out_own, out_arrived],
        scalars=1,
        after=[tails[0]],
    )
    results_here = over_tt(results)
    ffn_sum, ffn_second_new, ffn_new = run_kernel(
        6.9,
        unit_adam_kernel,
        [shape(ffn_rows_own, 3 * D)] * 3,
        [unit_sum, ffn_weights, ffn_first, ffn_second, jnp.asarray(ffn_rates())[None]],
        after=[results[0]],
    )
    tail, out_sum = run_kernel(
        2,
        sum_kernel,
        [low(SLOTS, attn_rows + GAIN_ROWS, HEAD_COLS), shape(attn_rows, QUERY_WIDTH)],
        cross_send(tails),
        after=[ffn_sum, proj_here],
    )
    tail_here = exchange(tail, ("zz", "core"))

    output, input_grad = run_kernel(
        300,
        functools.partial(last_kernel, tt_count, run),
        [shape(ctx_count, run, D), shape(ctx_count, run, D)],
        [place, order_table, proj_here, in_weights, norm_in] + packs_here + results_here,
        scratch=[
            pltpu.VMEM((rows, SLOTS * HEAD_COLS), BF16),
            pltpu.VMEM((rows, D), F32),
            pltpu.VMEM((rows, D), F32),
        ],
        scalars=2,
        after=[tail],
    )
    lanes = 2 * HEAD_SIZE
    attn_sum, attn_second_new, attn_new, gain_sum, gain_second_new, gain_new = run_kernel(
        2.8,
        attn_adam_kernel,
        [shape(attn_rows, 3 * D)] * 3 + [shape(gains.shape[0] // lanes, lanes)] * 3,
        [tail_here, out_sum]
        + [attn_weights, attn_first, attn_second, jnp.asarray(attention_rates())[None]]
        + [g.reshape(-1, lanes) for g in (gains, gain_first, gain_second)],
        after=[input_grad],
    )
    return (
        output.reshape(1, rows, D),
        input_grad.reshape(1, rows, D),
        attn_sum,
        attn_second_new,
        attn_new,
        ffn_sum,
        ffn_second_new,
        ffn_new,
        gain_sum.reshape(-1),
        gain_second_new.reshape(-1),
        gain_new.reshape(-1),
    )


def solution(mesh):
    ctx_count, fsdp_count = mesh.shape["ctx"], mesh.shape["fsdp"]
    fine = Mesh(mesh.devices.reshape(RINGS, ctx_count // SLOTS, 2, fsdp_count), ALL)
    tokens = P("fsdp", CTX, None)
    states = P(ALL, None)
    return jax.shard_map(
        on_device,
        mesh=fine,
        in_specs=(
            tokens,
            tokens,
            P("fsdp", None),
            P("fsdp", None, None),
            P("fsdp", CTX),
            *([states] * 6),
            *([P()] * 3),
        ),
        out_specs=(tokens, tokens, *([states] * 6), *([P()] * 3)),
        check_vma=False,
    )
```

```python
import functools
import math

import jax
import jax.numpy as jnp
import numpy as np
from jax import lax
from jax.experimental import pallas as pl
from jax.experimental.pallas import tpu as pltpu
from jax.sharding import Mesh, PartitionSpec as P

D = 1024
QUERY_HEADS = 16
KEY_VALUE_HEADS = 8
HEAD_SIZE = 64
FF = 4608
STEP = 10

QUERY_WIDTH = QUERY_HEADS * HEAD_SIZE
KEY_WIDTH = KEY_VALUE_HEADS * HEAD_SIZE
GROUP = QUERY_HEADS // KEY_VALUE_HEADS
PAIR = GROUP * HEAD_SIZE
HEAD_COLS = PAIR + 2 * HEAD_SIZE

EPSILON = 1e-05
ROPE_BASE = 1000000.0
SHIFT_FACTOR = 2.6
SCALE = HEAD_SIZE ** (-0.5)
SHIFT = SHIFT_FACTOR * HEAD_SIZE**0.5
LOG2E = math.log2(math.e)
BETA_FIRST = 0.9
BETA_SECOND = 0.999
ADAM_EPSILON = 1e-08
WEIGHT_DECAY = 0.01
GAIN_RATE = 0.8

BF16 = jnp.bfloat16
F32 = jnp.float32
I32 = jnp.int32
MIB = 1 << 20

def mm(left, right, left_dim, right_dim):
    return lax.dot_general(
        left, right, (((left_dim,), (right_dim,)), ((), ())), preferred_element_type=F32
    )


def rms_parts(values):
    factor = lax.rsqrt(jnp.mean(values * values, axis=-1, keepdims=True) + EPSILON)
    return (factor, values * factor)


def norm_back(grad_hat, unit_vals, factor):
    return factor * (grad_hat - unit_vals * jnp.mean(grad_hat * unit_vals, axis=-1, keepdims=True))


def attention_rates():
    return np.concatenate(
        [
            np.full((QUERY_WIDTH + 2 * KEY_WIDTH,), D ** (-0.5), np.float32),
            np.full((QUERY_WIDTH,), (QUERY_WIDTH / 16.0) ** (-0.5), np.float32),
        ]
    )


def ffn_rates():
    return np.concatenate(
        [np.full((2 * D,), D ** (-0.5), np.float32), np.full((D,), FF ** (-0.5), np.float32)]
    )


def adam_update(weight, gradient, first_moment, second, step_rate):
    first_new = BETA_FIRST * first_moment + (1.0 - BETA_FIRST) * gradient
    second_new = BETA_SECOND * second + (1.0 - BETA_SECOND) * gradient * gradient
    normalized = (
        first_new
        / (1.0 - BETA_FIRST**STEP)
        / (jnp.sqrt(second_new / (1.0 - BETA_SECOND**STEP)) + ADAM_EPSILON)
    )
    return (weight - step_rate * (normalized + WEIGHT_DECAY * weight), second_new)


RINGS = 4
SLOTS = 2 * RINGS
ALL = ("zz", "tt", "core", "fsdp")
CTX = ("zz", "tt", "core")
SLOT, ZZ, TT, CORE, FSDP = range(5)
GAIN_ROWS = 2 * D // HEAD_COLS + 1


def core_swap(block):
    return lax.ppermute(block, "core", [(0, 1), (1, 0)])


def zz_xor(block, k):
    return lax.ppermute(block, "zz", [(i, i ^ k) for i in range(RINGS)])


def tt_from(block, offset):
    count = lax.axis_size("tt")
    return lax.ppermute(block, "tt", [((i + offset) % count, i) for i in range(count)])


def exchange(blocks, axes):
    return lax.all_to_all(blocks, axes, split_axis=0, concat_axis=0, tiled=True)


def gather_from(copies):
    straight = exchange(copies, ("zz",))
    return [straight, core_swap(straight)]


def cross_send(parts):
    tt_count, fsdp_count = lax.axis_size("tt"), lax.axis_size("fsdp")
    if tt_count != 2 or fsdp_count != 2:
        came = exchange(jnp.stack(parts), ("tt", "fsdp"))
        return [came[n] for n in range(tt_count * fsdp_count)]
    pairs = [[(n, n ^ i) for n in range(4)] for i in range(4)]
    return [parts[0]] + [lax.ppermute(parts[i], ("tt", "fsdp"), pairs[i]) for i in (3, 1, 2)]


SMEM = pl.BlockSpec(memory_space=pltpu.SMEM)
VMEM = pl.BlockSpec(memory_space=pltpu.VMEM)
ANY = pl.BlockSpec(memory_space=pl.ANY)


STATED = 0.1
MXU_FLOPS = 1.15e9


def stated(micros):
    return pl.CostEstimate(
        flops=int(micros * STATED * MXU_FLOPS), bytes_accessed=1, transcendentals=0
    )


def run_kernel(micros, kernel, outs, args, scratch=(), scalars=0, after=(), limit=64):
    skip = len(after)
    return pl.pallas_call(
        lambda *refs: kernel(*refs[skip:]),
        out_shape=tuple(outs),
        in_specs=[ANY] * skip + [SMEM] * scalars + [VMEM] * (len(args) - scalars),
        out_specs=(VMEM,) * len(outs),
        scratch_shapes=list(scratch),
        compiler_params=pltpu.CompilerParams(vmem_limit_bytes=limit * MIB),
        cost_estimate=stated(micros),
    )(*after, *args)


def shape(*dims, dtype=F32):
    return jax.ShapeDtypeStruct(dims, dtype)


def low(*dims):
    return shape(*dims, dtype=BF16)


def at_row(index, rows):
    return pl.ds(pl.multiple_of(index * rows, rows), rows)


def lanes_of(rows):
    return lax.broadcasted_iota(I32, (rows, 2 * HEAD_SIZE), 1)


def swap_halves(values, lanes):
    half = HEAD_SIZE // 2
    return jnp.where(
        lanes % HEAD_SIZE < half,
        pltpu.roll(values, 2 * HEAD_SIZE - half, 1),
        pltpu.roll(values, half, 1),
    )


def widen(cosine, sine):
    return (
        jnp.concatenate([cosine] * 4, axis=1),
        jnp.concatenate([-sine, sine, -sine, sine], axis=1),
    )


def head_sums(values, lanes):
    left = jnp.sum(jnp.where(lanes < HEAD_SIZE, values, 0.0), axis=1, keepdims=True)
    right = jnp.sum(jnp.where(lanes < HEAD_SIZE, 0.0, values), axis=1, keepdims=True)
    return jnp.where(lanes < HEAD_SIZE, left, right)


def to_row(column):
    wide = jnp.broadcast_to(column, (column.shape[0], 2 * HEAD_SIZE))
    return jnp.transpose(wide)[:1]


def to_column(row):
    wide = jnp.broadcast_to(row, (2 * HEAD_SIZE, row.shape[1]))
    return jnp.transpose(wide)[:, :1]


def heads_kernel(attn_ref, heads_ref):
    keys = QUERY_WIDTH
    values = QUERY_WIDTH + KEY_WIDTH
    for h in range(SLOTS):
        heads_ref[h] = jnp.concatenate(
            [
                attn_ref[:, h * PAIR : (h + 1) * PAIR],
                attn_ref[:, keys + h * HEAD_SIZE : keys + (h + 1) * HEAD_SIZE],
                attn_ref[:, values + h * HEAD_SIZE : values + (h + 1) * HEAD_SIZE],
            ],
            axis=1,
        ).astype(BF16)


def units_kernel(ffn_ref, heads_ref, units_ref, in_ref):
    units_ref[...] = ffn_ref[...].astype(BF16)
    part = heads_ref.shape[1]
    per = D // HEAD_COLS
    for h in range(SLOTS):
        in_ref[
            (h // per) * part : (h // per + 1) * part,
            (h % per) * HEAD_COLS : (h % per + 1) * HEAD_COLS,
        ] = heads_ref[h]


def block_kernel(tokens_ref, weights_ref, block_ref):
    rows = tokens_ref.shape[0]
    block_ref[:rows] = tokens_ref[...]
    block_ref[rows:] = weights_ref[:, QUERY_WIDTH + 2 * KEY_WIDTH :].astype(BF16)


def repeat_kernel(heads_ref, copies_ref):
    for n in range(copies_ref.shape[0]):
        copies_ref[n] = heads_ref[...]


def token_kernel(tt_count, run, place_ref, order_ref, lengths_ref, *refs):
    key_row_ref, first_row_ref, position_ref, wide_ref = refs
    chunk = tt_count * 2 * SLOTS * run
    rows = tt_count * 2 * RINGS * run
    tt, core = place_ref[TT], place_ref[CORE]
    offsets = lax.broadcasted_iota(I32, (run, 2 * HEAD_SIZE), 0)
    for b in range(RINGS):
        for v in range(tt_count):
            group = lax.rem(tt + v, tt_count)
            for u in range(tt_count):
                for s in range(2):
                    block = (b * tt_count + lax.rem(group + u, tt_count)) * 2 + (core ^ s)
                    for slot in range(SLOTS):
                        sender = ((slot // 2) * tt_count + group) * 2 + slot % 2
                        start = block * rows + order_ref[block, sender] * run
                        base = v * chunk + ((u * 2 + s) * SLOTS + slot) * run
                        wide_ref[base : base + run] = (offsets + start).astype(F32)
        key_row_ref[b] = jnp.transpose(wide_ref[...])[:1]
        own = wide_ref[:chunk]
        first = jnp.zeros_like(own)
        begin = 0
        for k in range(lengths_ref.shape[0]):
            begin_f = jnp.full_like(own, begin).astype(F32)
            first = jnp.maximum(first, jnp.where(own >= begin_f, begin_f, 0.0))
            begin = begin + lengths_ref[k]
        first_row_ref[b] = jnp.transpose(first)[:1]
        position_ref[b * chunk : (b + 1) * chunk] = own[:, :1] - first[:, :1]


def cotangent_kernel(tt_count, run, place_ref, order_ref, cotangent_ref, mask_ref, *refs):
    own_ref, away_refs, masked_ref, sorted_ref = refs[0], refs[1:-2], refs[-2], refs[-1]
    rows = cotangent_ref.shape[0]
    mask = jnp.transpose(jnp.broadcast_to(mask_ref[...].astype(F32), (rows, rows)))[:, :1]
    masked = jnp.where(mask > 0.0, cotangent_ref[...].astype(F32), 0.0)
    masked_ref[...] = masked.reshape(masked_ref.shape)
    zz, tt, core = place_ref[ZZ], place_ref[TT], place_ref[CORE]
    block = (zz * tt_count + tt) * 2 + core
    for v in range(tt_count):
        group = lax.rem(tt + v, tt_count)
        for slot in range(SLOTS):
            sender = ((slot // 2) * tt_count + group) * 2 + slot % 2
            sorted_ref[slot * run : (slot + 1) * run] = masked_ref[order_ref[block, sender]]
        out_ref = own_ref if v == 0 else away_refs[v - 1]
        out_ref[...] = sorted_ref[...].astype(BF16)


def copies_kernel(*refs):
    part_refs, out_ref = refs[:-1], refs[-1]
    rows = part_refs[0].shape[0]
    for n in range(RINGS):
        for u, ref in enumerate(part_refs):
            out_ref[n, u * rows : (u + 1) * rows] = ref[...]


def project_kernel(tt_count, fsdp_count, run, place_ref, *refs):
    chunk_refs, parts_ref, refs = refs[:SLOTS], refs[SLOTS], refs[SLOTS + 1 :]
    norm_ref, gain_ref, cos_ref, sin_ref = refs[:4]
    inputs_ref, normed_ref, own_ref, query_ref, both_ref, linear_ref, weights_ref = refs[4:11]
    out_part_ref, wide_cos_ref, wide_sin_ref, sorted_ref, part_ref = refs[11:]
    rows = part_ref.shape[0] * run
    piece = SLOTS * run
    slot, zz, tt, core = (place_ref[i] for i in (SLOT, ZZ, TT, CORE))
    part_rows = parts_ref.shape[2]
    for n in range(parts_ref.shape[0]):
        t, f = n // fsdp_count, n % fsdp_count
        for m in range(SLOTS):
            device = (((m // 2) * tt_count + t) * 2 + m % 2) * fsdp_count + f
            weights_ref[device * part_rows : (device + 1) * part_rows] = parts_ref[n, m]
    for n in range(SLOTS):
        part_ref[...] = chunk_refs[n][:rows].astype(F32).reshape(part_ref.shape)
        out_part_ref[slot ^ n] = chunk_refs[n][rows:]
        for b in range(RINGS):
            for u in range(tt_count):
                for s in range(2):
                    block = (b * tt_count + lax.rem(tt + u, tt_count)) * 2 + (core ^ s)
                    base = ((b * tt_count + u) * 2 + s) * SLOTS + (slot ^ n)
                    sorted_ref[base] = part_ref[block]
    for u in range(tt_count):
        own = sorted_ref[pl.ds((zz * tt_count + u) * 2 * SLOTS, SLOTS)]
        own_ref[u * piece : (u + 1) * piece] = own.reshape(piece, D).astype(BF16)
    step = SLOTS * rows // RINGS
    lanes = lanes_of(step)
    key_part = lanes < HEAD_SIZE
    for a in range(RINGS):
        at = slice(a * step, (a + 1) * step)
        values = sorted_ref[a * step // run : (a + 1) * step // run].reshape(step, D)
        inputs_ref[at] = values.astype(BF16)
        normed = (rms_parts(values)[1] * norm_ref[...]).astype(BF16)
        normed_ref[at] = normed
        linear = mm(normed, weights_ref[...], 1, 0)
        linear_ref[at] = linear
        query, both = linear[:, :PAIR], linear[:, PAIR:]
        cosine, sine = widen(cos_ref[at], sin_ref[at])
        wide_cos_ref[at], wide_sin_ref[at] = cosine, sine
        query_factor = lax.rsqrt(head_sums(query * query, lanes) / HEAD_SIZE + EPSILON)
        query = query * query_factor * gain_ref[:, :PAIR]
        query = query * cosine + swap_halves(query, lanes) * sine
        query_ref[at] = query.astype(BF16)
        key_factor = lax.rsqrt(head_sums(both * both, lanes) / HEAD_SIZE + EPSILON)
        key = both * key_factor * gain_ref[:, PAIR:]
        key = key * cosine + swap_halves(key, lanes) * sine
        both_ref[at] = jnp.where(key_part, key, both).astype(BF16)


def spread_keys(both_refs, keys_ref, values_ref, chunk, filler):
    lanes = lanes_of(chunk)
    left = lanes < HEAD_SIZE
    for b in range(RINGS):
        for u, ref in enumerate(both_refs):
            both = ref[b * chunk : (b + 1) * chunk].astype(F32)
            turned = pltpu.roll(both, HEAD_SIZE, 1)
            at = slice(u * chunk, (u + 1) * chunk)
            keys_ref[b, at] = jnp.where(left, both, turned).astype(BF16)
            values_ref[b, 0, at] = jnp.where(left, turned, filler).astype(BF16)
            values_ref[b, 1, at] = jnp.where(left, filler, both).astype(BF16)


def one_head(values, lanes, head):
    keep = lanes < HEAD_SIZE if head == 0 else lanes >= HEAD_SIZE
    return jnp.where(keep, values, jnp.zeros_like(values))


def attend_kernel(tt_count, query_ref, *refs):
    both_refs, refs = refs[:tt_count], refs[tt_count:]
    key_row_ref, first_ref = refs[:2]
    mixed_low_ref, mixed_ref, totals_ref = refs[2:5]
    keys_ref, values_ref, numer_ref = refs[5:]
    chunk = query_ref.shape[0] // RINGS
    spread_keys(both_refs, keys_ref, values_ref, chunk, 1.0)
    lanes = lanes_of(chunk)
    for a in range(RINGS):
        at = slice(a * chunk, (a + 1) * chunk)
        query = query_ref[at]
        queries = [one_head(query, lanes, h) for h in range(GROUP)]
        token, first = to_column(key_row_ref[a, :, :chunk]), to_column(first_ref[a])
        numer_ref[...] = jnp.zeros_like(numer_ref)

        def add(b, visible):
            for h in range(GROUP):
                scores = mm(queries[h], keys_ref[b], 1, 1)
                weight = jnp.where(
                    visible, jnp.exp2(scores * (SCALE * LOG2E) - SHIFT * LOG2E), 0.0
                )
                numer_ref[h] += mm(weight.astype(BF16), values_ref[b, h], 1, 0)

        def below(b, carry):
            add(b, key_row_ref[b] >= first)
            return carry

        lax.fori_loop(0, a, below, 0)
        add(a, (key_row_ref[a] >= first) & (key_row_ref[a] <= token))
        numer = jnp.where(lanes < HEAD_SIZE, numer_ref[0], numer_ref[1])
        totals = pltpu.roll(
            jnp.where(lanes < HEAD_SIZE, numer_ref[1], numer_ref[0]), HEAD_SIZE, 1
        )
        mixed = numer / totals
        mixed_ref[at] = mixed
        mixed_low_ref[at] = mixed.astype(BF16)
        totals_ref[at] = totals


def turn(values):
    return jnp.transpose(values.astype(F32)).astype(BF16)


def out_weights_kernel(
    tt_count, fsdp_count, parts_ref, units_ref, passed_ref, out_ref, out_turned_ref, turned_ref, copy_ref
):
    rows = parts_ref.shape[2]
    for t in range(tt_count):
        for f in range(fsdp_count):
            for m in range(SLOTS):
                device = (((m // 2) * tt_count + t) * 2 + m % 2) * fsdp_count + f
                out_ref[device * rows : (device + 1) * rows] = parts_ref[t * fsdp_count + f, m]
    copy_ref[...] = passed_ref[...]
    step = 2 * PAIR
    for n in range(0, D, step):
        out_turned_ref[n : n + step] = turn(out_ref[:, n : n + step])
        for i in range(3):
            turned_ref[i, n : n + step] = turn(units_ref[:, i * D + n : i * D + n + step])


def in_weights_kernel(cross, parts_ref, out_ref):
    half = parts_ref.shape[2] // 2
    for n in range(2 * cross):
        for z in range(RINGS):
            device = z * 2 * cross + n
            at = slice(device * half, (device + 1) * half)
            out_ref[at, :D] = parts_ref[n, z, :half]
            out_ref[at, D:] = parts_ref[n, z, half:]


def feed_kernel(tt_count, first_k, skip, place_ref, *refs):
    refs = refs[skip:]
    mixed_refs, inputs_ref, cot_refs = refs[:2], refs[2], refs[3:5]
    out_turned_hbm, turned_hbm, units_hbm, norm_ref = refs[5:9]
    refs = refs[9:]
    hidden_ref, normed_ref, active_ref, gate_ref, up_ref, grad_ref = refs[:6]
    mid_own_ref, out_own_ref, out_away_ref, mid_away_refs = refs[6], refs[7], refs[8], refs[9:11]
    all_ref, grad_all_ref, out_turned_ref, turned_ref, units_ref = refs[11:16]
    hidden_all_ref, mid_ref, out_ref, sems = refs[16:]
    copies = [
        pltpu.make_async_copy(out_turned_hbm, out_turned_ref, sems.at[0]),
        pltpu.make_async_copy(turned_hbm, turned_ref, sems.at[1]),
        pltpu.make_async_copy(units_hbm, units_ref, sems.at[2]),
    ]
    for copy in copies:
        copy.start()
    rows = cot_refs[0].shape[1]
    piece = rows // tt_count
    zz, core = place_ref[ZZ], place_ref[CORE]
    for c in range(2):
        for z in range(RINGS):
            column = pl.ds(pl.multiple_of((z * 2 + (core ^ c)) * PAIR, PAIR), PAIR)
            for u in range(2 * tt_count):
                for s in range(2):
                    to = (u * 2 + s) * piece
                    source = (u * 2 + (s ^ c)) * piece
                    all_ref[to : to + piece, column] = mixed_refs[c][z, source : source + piece]
    for q in range(2):
        for u in range(tt_count):
            for s in range(2):
                to = ((q * tt_count + u) * 2 + s) * piece
                grad_all_ref[to : to + piece] = cot_refs[s][q, u * piece : (u + 1) * piece]
    copies[0].wait()
    hidden = inputs_ref[...].astype(F32) + mm(all_ref[...], out_turned_ref[...], 1, 0)
    hidden_all_ref[...] = hidden
    normed = (rms_parts(hidden)[1] * norm_ref[...]).astype(BF16)
    copies[1].wait()
    gate = mm(normed, turned_ref[0], 1, 0)
    up = mm(normed, turned_ref[1], 1, 0)
    sigmoid = 1.0 / (1.0 + jnp.exp(-gate))
    swish = gate * sigmoid
    active = (swish * up).astype(BF16)
    grad_act = mm(grad_all_ref[...], turned_ref[2], 1, 0)
    grad_up = (grad_act * swish).astype(BF16)
    grad_gate = (grad_act * up * sigmoid * (1.0 + gate * (1.0 - sigmoid))).astype(BF16)
    half = 2 * rows
    for q in range(2):
        at = slice(q * half, (q + 1) * half)
        normed_ref[q] = normed[at]
        active_ref[q] = active[at]
        gate_ref[q] = grad_gate[at]
        up_ref[q] = grad_up[at]
        grad_ref[q] = grad_all_ref[at]
    copies[2].wait()
    mid_ref[...] = mm(grad_gate, units_ref[:, :D], 1, 0) + mm(
        grad_up, units_ref[:, D : 2 * D], 1, 0
    )
    out_ref[...] = mm(active, units_ref[:, 2 * D :], 1, 0)
    for i in range(2):
        first = ((zz ^ (first_k - i)) % 2) * 2 * tt_count
        for u in range(tt_count):
            to = slice(u * piece, (u + 1) * piece)
            own, away = at_row(first + 2 * u, piece), at_row(first + 2 * u + 1, piece)
            if i == 1:
                hidden_ref[to] = hidden_all_ref[own]
            mid_own_ref[i, to] = mid_ref[own]
            out_own_ref[i, to] = out_ref[own]
            out_away_ref[i, to] = out_ref[away].astype(BF16)
            mid_away_refs[i][to] = mid_ref[away].astype(BF16)


def feed(
    first_k, steps, after, tt_count, place, mixed, inputs, cot, out_turned, turned, units, norm_mid
):
    rows = cot[0].shape[1]
    unit_count = units.shape[0]

    def pair(i, place):
        return (place[ZZ] // 2) ^ (first_k // 2)

    def whole(array):
        return pl.BlockSpec(array.shape, lambda i, place: (0,) * len(array.shape))

    hidden = shape(rows, D)
    outs = [
        low(steps, 2 * rows, D),
        low(steps, 2 * rows, unit_count),
        low(steps, 2 * rows, unit_count),
        low(steps, 2 * rows, unit_count),
        low(steps, 2 * rows, D),
        shape(steps, rows, D),
        shape(steps, rows, D),
        low(steps, rows, D),
    ]
    away = [low(rows, D)] * steps
    return pl.pallas_call(
        functools.partial(feed_kernel, tt_count, first_k, len(after)),
        out_shape=tuple([hidden] + outs + away),
        grid_spec=pltpu.PrefetchScalarGridSpec(
            num_scalar_prefetch=1,
            grid=(1,),
            in_specs=[ANY] * len(after)
            + [
                pl.BlockSpec((RINGS, 4 * rows, PAIR), lambda i, p: (0, pair(i, p), 0)),
                pl.BlockSpec((RINGS, 4 * rows, PAIR), lambda i, p: (0, pair(i, p), 0)),
                pl.BlockSpec((4 * rows, D), lambda i, p: (pair(i, p), 0)),
                pl.BlockSpec((2, rows, D), lambda i, p: (pair(i, p), 0, 0)),
                pl.BlockSpec((2, rows, D), lambda i, p: (pair(i, p), 0, 0)),
                ANY,
                ANY,
                ANY,
                whole(norm_mid),
            ],
            out_specs=tuple(whole(o) for o in [hidden] + outs + away),
            scratch_shapes=[
                pltpu.VMEM((4 * rows, QUERY_WIDTH), BF16),
                pltpu.VMEM((4 * rows, D), BF16),
                pltpu.VMEM(out_turned.shape, BF16),
                pltpu.VMEM(turned.shape, BF16),
                pltpu.VMEM(units.shape, BF16),
                pltpu.VMEM((4 * rows, D), F32),
                pltpu.VMEM((4 * rows, D), F32),
                pltpu.VMEM((4 * rows, D), F32),
                pltpu.SemaphoreType.DMA((3,)),
            ],
        ),
        compiler_params=pltpu.CompilerParams(vmem_limit_bytes=64 * MIB),
        cost_estimate=stated(14),
    )(place, *after, *mixed, inputs, *cot, out_turned, turned, units, norm_mid)


def far_kernel(own_ref, swapped_far_ref, swapped_next_ref, passed_ref, sum_ref, copy_ref):
    for n, ref in enumerate((swapped_far_ref, swapped_next_ref)):
        sum_ref[n] = (own_ref[n] + ref[...].astype(F32)).astype(BF16)
    copy_ref[...] = passed_ref[...]


def next_kernel(own_ref, swapped_ref, far_ref, sum_ref):
    total = own_ref[0] + swapped_ref[...].astype(F32) + far_ref[0].astype(F32)
    sum_ref[...] = total.astype(BF16)


def middle_kernel(tt_count, *refs):
    own_ref, swapped_ref, far_ref, next_ref, refs = *refs[:4], refs[4:]
    hidden_ref, cot_ref, out_weights_ref, norm_ref = refs[:4]
    inputs_ref, refs = refs[4], refs[5:]
    send_ref, gain_ref, pack_refs = refs[0], refs[1], refs[2:]
    grad_mid = own_ref[1] + swapped_ref[...].astype(F32)
    grad_mid += far_ref[1].astype(F32) + next_ref[...].astype(F32)
    factor, unit = rms_parts(hidden_ref[...])
    gain_ref[...] = jnp.sum(grad_mid * unit, axis=0, keepdims=True)
    grad_hidden = cot_ref[...].astype(F32) + norm_back(grad_mid * norm_ref[...], unit, factor)
    hidden_low = grad_hidden.astype(BF16)
    piece = pack_refs[0].shape[1]
    for u, ref in enumerate(pack_refs):
        at = slice(u * piece, (u + 1) * piece)
        ref[0] = inputs_ref[at]
        ref[1] = hidden_low[at]
    grad_mixed = mm(hidden_low, out_weights_ref[...], 1, 0).astype(BF16)
    width = (send_ref.shape[2] - PAIR) // tt_count
    for n in range(SLOTS):
        send_ref[n, :, :PAIR] = grad_mixed[:, n * PAIR : (n + 1) * PAIR]
        parts = []
        for t in range(tt_count):
            base = (((n // 2) * tt_count + t) * 2 + n % 2) * width
            parts.append(grad_hidden[:, base : base + width])
        send_ref[n, :, PAIR:] = jnp.concatenate(parts, axis=1).astype(BF16)


def out_sum_kernel(place_ref, own_far, own_near, swapped_far, swapped_near, send_ref, here_ref):
    zz = place_ref[ZZ]
    for k in range(RINGS):
        own, swapped = (own_far, swapped_far) if k > 1 else (own_near, swapped_near)
        total = own[1 - k % 2] + swapped[1 - k % 2].astype(F32)
        send_ref[zz ^ k] = total.astype(BF16)
        if k == 0:
            here_ref[...] = total


def result_kernel(place_ref, hidden_ref, own_ref, arrived_ref, *pack_refs):
    zz = place_ref[ZZ]
    result = hidden_ref[...] + own_ref[...]
    for k in range(1, RINGS):
        result += arrived_ref[zz ^ k].astype(F32)
    result = result.astype(BF16)
    piece = pack_refs[0].shape[0]
    for u, ref in enumerate(pack_refs):
        ref[...] = result[u * piece : (u + 1) * piece]


def attend_back_kernel(tt_count, place_ref, query_ref, *refs):
    both_refs, refs = refs[:tt_count], refs[tt_count:]
    grad_mixed_ref, mixed_ref, totals_ref = refs[:3]
    key_row_ref, first_ref = refs[3:5]
    grad_query_ref, grad_own_ref, refs = refs[5], refs[6], refs[7:]
    grad_away_refs, refs = refs[: tt_count - 1], refs[tt_count - 1 :]
    keys_ref, values_ref, turned_ref, grad_both_ref, sorted_ref, query_sum_ref, column_ref = refs
    total = query_ref.shape[0]
    chunk = total // RINGS
    piece = total // SLOTS // tt_count
    spread_keys(both_refs, keys_ref, values_ref, chunk, -1.0)
    key_count = tt_count * chunk
    for b in range(RINGS):
        turned_ref[b] = jnp.transpose(keys_ref[b].astype(F32)[:, :HEAD_SIZE]).astype(BF16)
        column_ref[b] = to_column(key_row_ref[b])
    grad_both_ref[...] = jnp.zeros_like(grad_both_ref)
    core = place_ref[CORE]
    for n in range(SLOTS):
        for u in range(tt_count):
            to = ((n // 2) * tt_count + u) * 2 + (core ^ (n % 2))
            sorted_ref[at_row(to, piece)] = grad_mixed_ref[
                n, u * piece : (u + 1) * piece, :PAIR
            ].astype(F32)
    lanes = lanes_of(chunk)
    left = lanes < HEAD_SIZE
    for a in range(RINGS):
        at = slice(a * chunk, (a + 1) * chunk)
        query = query_ref[at]
        grad_mixed, totals = sorted_ref[at], totals_ref[at]
        grad_numer = (grad_mixed / totals).astype(BF16).astype(F32)
        delta = head_sums(grad_mixed * mixed_ref[at], lanes) / totals
        high = delta.astype(BF16).astype(F32)
        middle = (delta - high).astype(BF16).astype(F32)
        parts = jnp.where(
            lanes % HEAD_SIZE == 0,
            high,
            jnp.where(
                lanes % HEAD_SIZE == 1,
                middle,
                jnp.where(lanes % HEAD_SIZE == 2, delta - high - middle, 0.0),
            ),
        )
        parts = pltpu.roll(parts, HEAD_SIZE, 1)
        query_f = query.astype(F32)
        query_turned = pltpu.roll(query_f, HEAD_SIZE, 1)
        numer_turned = pltpu.roll(grad_numer, HEAD_SIZE, 1)
        queries = [one_head(query, lanes, h) for h in range(GROUP)]
        grads = [
            jnp.where(left, grad_numer, parts).astype(BF16),
            jnp.where(left, parts, grad_numer).astype(BF16),
        ]
        query_left = [
            jnp.where(left, query_f, 0.0).astype(BF16),
            jnp.where(left, query_turned, 0.0).astype(BF16),
        ]
        numer_right = [
            jnp.where(left, 0.0, numer_turned).astype(BF16),
            jnp.where(left, 0.0, grad_numer).astype(BF16),
        ]
        token, first = key_row_ref[a][:, :chunk], first_ref[a]
        query_sum_ref[...] = jnp.zeros_like(query_sum_ref)

        def add(b, visible):
            added = jnp.zeros((key_count, 2 * HEAD_SIZE), F32)
            for h in range(GROUP):
                scores = mm(keys_ref[b], queries[h], 1, 1)
                weight = jnp.where(
                    visible, jnp.exp2(scores * (SCALE * LOG2E) - SHIFT * LOG2E), 0.0
                )
                grad_weight = mm(values_ref[b, h], grads[h], 1, 1)
                grad_score = (weight * grad_weight).astype(BF16)
                added += mm(grad_score, query_left[h], 1, 0)
                added += mm(weight.astype(BF16), numer_right[h], 1, 0)
                query_sum_ref[h] += mm(turned_ref[b], grad_score, 1, 0)
            grad_both_ref[b] += added

        def below(b, carry):
            add(b, column_ref[b] >= first)
            return carry

        lax.fori_loop(0, a, below, 0)
        add(a, (column_ref[a] >= first) & (column_ref[a] <= token))
        grad_query_ref[at] = SCALE * jnp.transpose(
            jnp.concatenate([query_sum_ref[0], query_sum_ref[1]], axis=0)
        )
    for b in range(RINGS):
        at = slice(b * chunk, (b + 1) * chunk)
        for u in range(tt_count):
            part = grad_both_ref[b, u * chunk : (u + 1) * chunk]
            part = jnp.where(left, part * SCALE, part)
            if u == 0:
                grad_own_ref[at] = part
            else:
                grad_away_refs[u - 1][at] = part.astype(BF16)


def project_back_kernel(tt_count, place_ref, linear_ref, grad_query_ref, grad_own_ref, *refs):
    arrived_refs, refs = refs[: tt_count - 1], refs[tt_count - 1 :]
    gain_ref, cos_ref, sin_ref, proj_ref, grad_ref, gains_ref = refs
    total = grad_query_ref.shape[0]
    step = total // RINGS
    piece = step // tt_count // 2
    lanes = lanes_of(step)
    key_part = lanes < HEAD_SIZE
    tt, core = place_ref[TT], place_ref[CORE]
    sums = jnp.zeros((1, HEAD_COLS), F32)
    for a in range(RINGS):
        at = slice(a * step, (a + 1) * step)
        linear = linear_ref[at]
        cosine, sine = cos_ref[at], sin_ref[at]
        grad_both = grad_own_ref[at]
        for ref in arrived_refs:
            grad_both += ref[at].astype(F32)
        parts, gains = [], []
        for grad, values, gain in (
            (grad_query_ref[at], linear[:, :PAIR], gain_ref[:, :PAIR]),
            (grad_both, linear[:, PAIR:], gain_ref[:, PAIR:]),
        ):
            factor = lax.rsqrt(head_sums(values * values, lanes) / HEAD_SIZE + EPSILON)
            unit = values * factor
            grad_norm = grad * cosine - swap_halves(grad, lanes) * sine
            gains.append(jnp.sum(grad_norm * unit, axis=0, keepdims=True))
            hat = grad_norm * gain
            mean = head_sums(hat * unit, lanes) / HEAD_SIZE
            parts.append(factor * (hat - unit * mean))
        parts[1] = jnp.where(key_part, parts[1], grad_both)
        grad_low = jnp.concatenate(parts, axis=1).astype(BF16)
        grad_ref[at] = grad_low
        for u in range(tt_count):
            for s in range(2):
                block = (a * tt_count + lax.rem(tt + u, tt_count)) * 2 + (core ^ s)
                base = (u * 2 + s) * piece
                proj_ref[block] = grad_low[base : base + piece]
        sums += jnp.concatenate(gains, axis=1)
    gains_ref[...] = sums


def head_grad_kernel(tt_count, fsdp_count, relative, place_ref, *refs):
    normed_ref, grad_ref, weights_ref, norm_ref, mid_ref, head_ref, out_grad_ref = refs[:7]
    out_refs, product_ref = refs[7:-1], refs[-1]
    rows = out_grad_ref.shape[0] // tt_count // fsdp_count
    half = rows // 2
    tt, fsdp = place_ref[TT], place_ref[FSDP]
    product_ref[...] = mm(normed_ref[...], grad_ref[...], 0, 0)
    column = jnp.sum(product_ref[...] * weights_ref[...].astype(F32), axis=1, keepdims=True)
    gain_in = to_row(column) / norm_ref[...]
    parts = [
        row[:, i : i + HEAD_COLS]
        for row in (gain_in, mid_ref[...], head_ref[...])
        for i in range(0, row.shape[1], HEAD_COLS)
    ]
    gains = jnp.concatenate(parts, axis=0)
    for n, out_ref in enumerate(out_refs):
        t, f = n // fsdp_count, n % fsdp_count
        if relative:
            t, f = t ^ tt, f ^ fsdp
        for m in range(SLOTS):
            device = (((m // 2) * tt_count + t) * 2 + m % 2) * fsdp_count + f
            part = product_ref[at_row(device, rows)]
            out = out_grad_ref[
                at_row(t * fsdp_count + f, rows), (m % 4) * HEAD_COLS : (m % 4 + 1) * HEAD_COLS
            ][(m // 4) * half : (m // 4 + 1) * half]
            out_ref[m] = jnp.concatenate([part, out, gains], axis=0).astype(BF16)


def sum_kernel(*refs):
    part_refs, tail_ref, out_ref = refs[:-2], refs[-2], refs[-1]
    rows = out_ref.shape[0]
    half = rows // 2
    for m in range(SLOTS):
        total = part_refs[0][m].astype(F32)
        for ref in part_refs[1:]:
            total += ref[m].astype(F32)
        tail_ref[m] = jnp.concatenate([total[:rows], total[rows + half :]], axis=0).astype(BF16)
        out_ref[
            (m // 4) * half : (m // 4 + 1) * half, (m % 4) * HEAD_COLS : (m % 4 + 1) * HEAD_COLS
        ] = total[rows : rows + half]


def out_grad_kernel(tt_count, place_ref, *refs):
    mixed_refs, columns_ref, product_ref, turned_ref = refs[:2], refs[2], refs[3], refs[4]
    total = mixed_refs[0].shape[1]
    piece = total // SLOTS // tt_count
    core = place_ref[CORE]
    for n in range(SLOTS):
        for u in range(tt_count):
            part = columns_ref[n, u * piece : (u + 1) * piece, PAIR:]
            for c in range(2):
                to = ((n // 2) * tt_count + u) * 2 + (core ^ c ^ (n % 2))
                turned_ref[c, at_row(to, piece)] = part
    for c in range(2):
        turned = jnp.transpose(turned_ref[c].astype(F32)).astype(BF16)
        for z in range(RINGS):
            column = pl.ds(pl.multiple_of((z * 2 + (core ^ c)) * PAIR, PAIR), PAIR)
            product_ref[:, column] = mm(turned, mixed_refs[c][z], 1, 0)


def unit_grad_kernel(*refs):
    fed, out_ref = (refs[:5], refs[5:10]), refs[10]
    rows_ref, product_ref, normed_ref, grad_ref = refs[-4:]
    step = fed[0][0].shape[1]

    def collect(index, to_ref):
        at = 0
        for call in fed:
            for i in range(call[index].shape[0]):
                to_ref[at : at + step] = call[index][i]
                at += step

    collect(0, normed_ref)
    collect(4, grad_ref)
    for index, other_ref, column in ((2, normed_ref, 0), (3, normed_ref, D), (1, grad_ref, 2 * D)):
        collect(index, rows_ref)
        product_ref[...] = mm(rows_ref[...], other_ref[...], 0, 0)
        out_ref[:, column : column + D] = product_ref[...].astype(BF16)


def unit_adam_kernel(*refs):
    grad_refs, refs = refs[:-7], refs[-7:]
    weight_ref, first_ref, second_ref, rate_ref, grad_ref, second_new_ref, new_ref = refs
    grad = grad_refs[0][...].astype(F32)
    for ref in grad_refs[1:]:
        grad += ref[...].astype(F32)
    grad_ref[...] = grad
    new, second_new = adam_update(
        weight_ref[...], grad, first_ref[...], second_ref[...], rate_ref[...]
    )
    new_ref[...] = new
    second_new_ref[...] = second_new


def attn_adam_kernel(tail_ref, out_ref, *refs):
    weight_ref, first_ref, second_ref, rate_ref = refs[:4]
    gains_ref, gain_first_ref, gain_second_ref = refs[4:7]
    grad_ref, second_new_ref, new_ref = refs[7:10]
    gain_grad_ref, gain_second_new_ref, gain_new_ref = refs[10:]
    rows = weight_ref.shape[0]
    queries, keys, values = [], [], []
    gains = jnp.zeros((GAIN_ROWS, HEAD_COLS), F32)
    for n in range(SLOTS):
        part = tail_ref[n].astype(F32)
        gains += part[rows:]
        queries.append(part[:rows, :PAIR])
        keys.append(part[:rows, PAIR : PAIR + HEAD_SIZE])
        values.append(part[:rows, PAIR + HEAD_SIZE :])
    grad = jnp.concatenate(queries + keys + values + [out_ref[...]], axis=1)
    grad_ref[...] = grad
    new, second_new = adam_update(
        weight_ref[...], grad, first_ref[...], second_ref[...], rate_ref[...]
    )
    new_ref[...] = new
    second_new_ref[...] = second_new
    lanes = gains_ref.shape[1]
    per = 2 * D // HEAD_COLS
    lines = [
        gains[i : i + 1, j : j + lanes] for i in range(per) for j in range(0, HEAD_COLS, lanes)
    ]
    heads = gains[per : per + 1]
    query = heads[:, :HEAD_SIZE] + heads[:, HEAD_SIZE:PAIR]
    lines.append(jnp.concatenate([query, heads[:, PAIR : PAIR + HEAD_SIZE]], axis=1))
    gain_grad = jnp.concatenate(lines, axis=0)
    gain_grad_ref[...] = gain_grad
    new, second_new = adam_update(
        gains_ref[...], gain_grad, gain_first_ref[...], gain_second_ref[...], GAIN_RATE
    )
    gain_new_ref[...] = new
    gain_second_new_ref[...] = second_new


def last_kernel(tt_count, run, place_ref, order_ref, proj_ref, weights_ref, norm_ref, *refs):
    pack_refs, result_refs, refs = refs[:tt_count], refs[tt_count : 2 * tt_count], refs[2 * tt_count :]
    output_ref, grad_ref, left_ref, inputs_ref, hidden_ref = refs
    piece = SLOTS * run
    zz, tt, core = place_ref[ZZ], place_ref[TT], place_ref[CORE]
    for v in range(tt_count):
        at = slice(v * piece, (v + 1) * piece)
        group = lax.rem(tt + v, tt_count)
        for h in range(SLOTS):
            source = ((h // 2) * tt_count + group) * 2 + h % 2
            left_ref[at, h * HEAD_COLS : (h + 1) * HEAD_COLS] = proj_ref[source]
        inputs_ref[at] = pack_refs[v][0].astype(F32)
        hidden_ref[at] = pack_refs[v][1].astype(F32)
    grad_normed = mm(left_ref[...], weights_ref[...], 1, 1)
    factor, unit = rms_parts(inputs_ref[...])
    back = hidden_ref[...] + norm_back(grad_normed * norm_ref[...], unit, factor)
    block = (zz * tt_count + tt) * 2 + core
    for v in range(tt_count):
        group = lax.rem(tt + v, tt_count)
        result = result_refs[v][...].astype(F32)
        for slot in range(SLOTS):
            sender = ((slot // 2) * tt_count + group) * 2 + slot % 2
            to = order_ref[block, sender]
            base = (v * SLOTS + slot) * run
            output_ref[to] = result[slot * run : (slot + 1) * run]
            grad_ref[to] = back[base : base + run]


def on_device(
    inputs,
    cotangent,
    lengths,
    order,
    pad_mask,
    attn_weights,
    attn_first,
    attn_second,
    ffn_weights,
    ffn_first,
    ffn_second,
    gains,
    gain_first,
    gain_second,
):
    zz, tt, core = lax.axis_index("zz"), lax.axis_index("tt"), lax.axis_index("core")
    fsdp = lax.axis_index("fsdp")
    tt_count, fsdp_count = lax.axis_size("tt"), lax.axis_size("fsdp")
    ctx_count = SLOTS * tt_count
    device_count = ctx_count * fsdp_count
    cross = tt_count * fsdp_count
    square = tt_count == 2 and fsdp_count == 2
    rows = inputs.shape[1]
    run = rows // ctx_count
    piece = SLOTS * run
    group_rows = SLOTS * rows
    chunk = group_rows // RINGS
    key_count = tt_count * chunk
    attn_rows, ffn_rows_own = attn_weights.shape[0], ffn_weights.shape[0]
    unit_count = ffn_rows_own * cross
    place = jnp.stack([zz * 2 + core, zz, tt, core, fsdp]).astype(I32)
    order_table, length_row = order[0], lengths[0]

    norm_in, norm_mid = gains[None, :D], gains[None, D : 2 * D]
    query_gain = gains[2 * D : 2 * D + HEAD_SIZE]
    key_gain = gains[2 * D + HEAD_SIZE :]
    head_gains = jnp.concatenate([query_gain] * GROUP + [key_gain, jnp.ones_like(key_gain)])[None]

    def over_tt(parts):
        return [parts[0]] + [tt_from(parts[tt_count - u], u) for u in range(1, tt_count)]

    (block_own,) = run_kernel(
        1, block_kernel, [low(rows + attn_rows, D)], [inputs[0], attn_weights]
    )
    (heads_low,) = run_kernel(
        1,
        heads_kernel,
        [low(SLOTS, attn_rows, HEAD_COLS)],
        [attn_weights],
        after=[block_own],
    )
    head_own = exchange(heads_low, ("zz", "core"))
    units_own, in_low = run_kernel(
        2,
        units_kernel,
        [low(ffn_rows_own, 3 * D), low(2 * attn_rows, D)],
        [ffn_weights, heads_low],
    )
    cot = run_kernel(
        1.8,
        functools.partial(cotangent_kernel, tt_count, run),
        [low(piece, D)] * tt_count,
        [place, order_table, cotangent[0], pad_mask],
        scratch=[pltpu.VMEM((ctx_count, run, D), F32), pltpu.VMEM((piece, D), F32)],
        scalars=2,
        after=[units_own],
    )
    (head_copies,) = run_kernel(
        0, repeat_kernel, [low(cross, SLOTS, attn_rows, HEAD_COLS)], [head_own]
    )
    straight = [block_own] + [zz_xor(block_own, k) for k in range(1, RINGS)]
    input_parts = [b for part in straight for b in (part, core_swap(part))]
    head_parts = exchange(head_copies, ("tt", "fsdp"))
    key_row, first_row, position = run_kernel(
        2.3,
        functools.partial(token_kernel, tt_count, run),
        [shape(RINGS, 1, key_count), shape(RINGS, 1, chunk), shape(group_rows, 1)],
        [place, order_table, length_row],
        scratch=[pltpu.VMEM((key_count, 2 * HEAD_SIZE), F32)],
        scalars=3,
        after=[cot[0]],
    )

    units = lax.all_gather(units_own, ("tt", "fsdp"), axis=0, tiled=True)
    frequency = jnp.exp(
        jnp.arange(HEAD_SIZE // 2, dtype=F32) * (-2.0 * math.log(ROPE_BASE) / HEAD_SIZE)
    )
    angles = position * frequency[None, :]
    cosine, sine = jnp.cos(angles), jnp.sin(angles)

    (cot_copies,) = run_kernel(
        2,
        copies_kernel,
        [low(RINGS, rows, D)],
        over_tt(cot),
        after=[key_row, cosine, sine] + [straight[k] for k in range(1, RINGS)],
    )
    cot_straight = exchange(cot_copies, ("zz",))
    inputs_sorted, normed, inputs_own, query, both, linear, head_weights, out_part, *table = run_kernel(
        50,
        functools.partial(project_kernel, tt_count, fsdp_count, run),
        [
            low(group_rows, D),
            low(group_rows, D),
            low(rows, D),
            low(group_rows, PAIR),
            low(group_rows, 2 * HEAD_SIZE),
            shape(group_rows, HEAD_COLS),
            low(D, HEAD_COLS),
            low(SLOTS, attn_rows, QUERY_WIDTH),
            shape(group_rows, PAIR),
            shape(group_rows, PAIR),
        ],
        [place] + input_parts + [head_parts, norm_in, head_gains, cosine, sine],
        scratch=[
            pltpu.VMEM((group_rows // run, run, D), F32),
            pltpu.VMEM((ctx_count, run, D), F32),
        ],
        scalars=1,
        after=[cot_copies],
    )
    both_sets = [both] + [tt_from(both, u) for u in range(1, tt_count)]
    out_parts = lax.all_gather(out_part, ("tt", "fsdp"), axis=0)

    key_scratch = pltpu.VMEM((RINGS, key_count, 2 * HEAD_SIZE), BF16)
    value_scratch = pltpu.VMEM((RINGS, GROUP, key_count, 2 * HEAD_SIZE), BF16)
    mixed_low, mixed, totals = run_kernel(
        0,
        functools.partial(attend_kernel, tt_count),
        [low(group_rows, PAIR), shape(group_rows, PAIR), shape(group_rows, PAIR)],
        [query] + both_sets + [key_row, first_row],
        scratch=[
            key_scratch,
            value_scratch,
            pltpu.VMEM((GROUP, chunk, PAIR), F32),
        ],
    )
    (mixed_copies,) = run_kernel(
        0,
        copies_kernel,
        [low(RINGS, group_rows, PAIR)],
        [mixed_low],
        after=[cot_straight, units],
    )
    mixed_parts = gather_from(mixed_copies)
    out_weights, out_turned, units_turned, cot_straight = run_kernel(
        2,
        functools.partial(out_weights_kernel, tt_count, fsdp_count),
        [
            low(D, QUERY_WIDTH),
            low(QUERY_WIDTH, D),
            low(3, D, unit_count),
            low(RINGS, rows, D),
        ],
        [out_parts, units, cot_straight],
        after=[mixed_copies],
    )
    cot_parts = [cot_straight, core_swap(cot_straight)]
    (in_copies,) = run_kernel(
        0, copies_kernel, [low(RINGS, 2 * attn_rows, D)], [in_low], after=[mixed_parts[0]]
    )
    in_straight = exchange(in_copies, ("zz",))

    def feed_half(first_k, after):
        return feed(
            first_k,
            2,
            after,
            tt_count,
            place,
            mixed_parts,
            inputs_sorted,
            cot_parts,
            out_turned,
            units_turned,
            units,
            norm_mid,
        )

    far = feed_half(3, [in_copies])
    far_sums, in_straight = run_kernel(
        0,
        far_kernel,
        [low(2, rows, D), low(*in_straight.shape)],
        [far[6], core_swap(far[9]), core_swap(far[10]), in_straight],
    )
    far_arrived = zz_xor(far_sums, 2)
    in_parts = lax.all_gather(in_straight, ("tt", "core", "fsdp"), axis=0)
    near = feed_half(1, [far_sums])
    swapped = [core_swap(near[9]), core_swap(near[10])]
    (unit_grad,) = run_kernel(
        0,
        unit_grad_kernel,
        [low(unit_count, 3 * D)],
        [half[i] for half in (far, near) for i in (1, 2, 3, 4, 5)],
        scratch=[
            pltpu.VMEM((group_rows, unit_count), BF16),
            pltpu.VMEM((unit_count, D), F32),
            pltpu.VMEM((group_rows, D), BF16),
            pltpu.VMEM((group_rows, D), BF16),
        ],
    )
    unit_sum = lax.psum_scatter(unit_grad, ("tt", "fsdp"), scatter_dimension=0, tiled=True)

    (next_sum,) = run_kernel(
        0,
        next_kernel,
        [low(rows, D)],
        [near[6], swapped[0], far_arrived],
        after=[unit_grad],
    )
    next_arrived = zz_xor(next_sum, 1)
    hidden_own = near[0]
    cot_own = cot_copies[0]
    mixed_send, gain_mid, *packs = run_kernel(
        4,
        functools.partial(middle_kernel, tt_count),
        [low(SLOTS, rows, PAIR + cross * attn_rows), shape(1, D)] + [low(2, piece, D)] * tt_count,
        [near[6], swapped[1], far_arrived, next_arrived]
        + [hidden_own, cot_own, out_weights, norm_mid, inputs_own],
    )
    mixed_here = exchange(mixed_send, ("zz", "core"))
    packs_here = over_tt(packs)

    (in_weights,) = run_kernel(
        0,
        functools.partial(in_weights_kernel, cross),
        [low(D, SLOTS * HEAD_COLS)],
        [in_parts],
        after=[mixed_send],
    )
    out_send, out_own = run_kernel(
        0,
        out_sum_kernel,
        [low(RINGS, rows, D), shape(rows, D)],
        [place, far[7], near[7], core_swap(far[8]), core_swap(near[8])],
        scalars=1,
        after=[in_weights],
    )
    out_arrived = exchange(out_send, ("zz",))

    back = run_kernel(
        1000,
        functools.partial(attend_back_kernel, tt_count),
        [shape(group_rows, PAIR), shape(group_rows, 2 * HEAD_SIZE)]
        + [low(group_rows, 2 * HEAD_SIZE)] * (tt_count - 1),
        [place, query] + both_sets + [mixed_here, mixed, totals, key_row, first_row],
        scratch=[
            key_scratch,
            value_scratch,
            pltpu.VMEM((RINGS, HEAD_SIZE, key_count), BF16),
            pltpu.VMEM((RINGS, key_count, 2 * HEAD_SIZE), F32),
            pltpu.VMEM((group_rows, PAIR), F32),
            pltpu.VMEM((GROUP, HEAD_SIZE, chunk), F32),
            pltpu.VMEM((RINGS, key_count, 1), F32),
        ],
        scalars=1,
        after=[out_send] + packs_here[1:],
    )
    arrived_both = over_tt(back[1:])[1:]
    (out_grad,) = run_kernel(
        3.3,
        functools.partial(out_grad_kernel, tt_count),
        [shape(cross * attn_rows, QUERY_WIDTH)],
        [place] + mixed_parts + [mixed_here],
        scratch=[pltpu.VMEM((2, group_rows, cross * attn_rows), BF16)],
        scalars=1,
        after=[back[0]],
    )
    proj, grad_proj, head_gain = run_kernel(
        5,
        functools.partial(project_back_kernel, tt_count),
        [low(ctx_count, piece, HEAD_COLS), low(group_rows, HEAD_COLS), shape(1, HEAD_COLS)],
        [place, linear, back[0], back[1]] + arrived_both + [head_gains] + table,
        scalars=1,
        after=[out_grad],
    )
    tails = run_kernel(
        4,
        functools.partial(head_grad_kernel, tt_count, fsdp_count, square),
        [low(SLOTS, attn_rows + attn_rows // 2 + GAIN_ROWS, HEAD_COLS)] * cross,
        [place, normed, grad_proj, head_weights, norm_in, gain_mid, head_gain, out_grad],
        scratch=[pltpu.VMEM((D, HEAD_COLS), F32)],
        scalars=1,
    )
    proj_here = exchange(proj, CTX)
    results = run_kernel(
        2.6,
        result_kernel,
        [low(piece, D)] * tt_count,
        [place, hidden_own, out_own, out_arrived],
        scalars=1,
        after=[tails[0]],
    )
    results_here = over_tt(results)
    ffn_sum, ffn_second_new, ffn_new = run_kernel(
        6.9,
        unit_adam_kernel,
        [shape(ffn_rows_own, 3 * D)] * 3,
        [unit_sum, ffn_weights, ffn_first, ffn_second, jnp.asarray(ffn_rates())[None]],
        after=[results[0]],
    )
    tail, out_sum = run_kernel(
        2,
        sum_kernel,
        [low(SLOTS, attn_rows + GAIN_ROWS, HEAD_COLS), shape(attn_rows, QUERY_WIDTH)],
        cross_send(tails),
        after=[ffn_sum, proj_here],
    )
    tail_here = exchange(tail, ("zz", "core"))

    output, input_grad = run_kernel(
        300,
        functools.partial(last_kernel, tt_count, run),
        [shape(ctx_count, run, D), shape(ctx_count, run, D)],
        [place, order_table, proj_here, in_weights, norm_in] + packs_here + results_here,
        scratch=[
            pltpu.VMEM((rows, SLOTS * HEAD_COLS), BF16),
            pltpu.VMEM((rows, D), F32),
            pltpu.VMEM((rows, D), F32),
        ],
        scalars=2,
        after=[tail],
    )
    lanes = 2 * HEAD_SIZE
    attn_sum, attn_second_new, attn_new, gain_sum, gain_second_new, gain_new = run_kernel(
        2.8,
        attn_adam_kernel,
        [shape(attn_rows, 3 * D)] * 3 + [shape(gains.shape[0] // lanes, lanes)] * 3,
        [tail_here, out_sum]
        + [attn_weights, attn_first, attn_second, jnp.asarray(attention_rates())[None]]
        + [g.reshape(-1, lanes) for g in (gains, gain_first, gain_second)],
        after=[input_grad],
    )
    return (
        output.reshape(1, rows, D),
        input_grad.reshape(1, rows, D),
        attn_sum,
        attn_second_new,
        attn_new,
        ffn_sum,
        ffn_second_new,
        ffn_new,
        gain_sum.reshape(-1),
        gain_second_new.reshape(-1),
        gain_new.reshape(-1),
    )


def solution(mesh):
    ctx_count, fsdp_count = mesh.shape["ctx"], mesh.shape["fsdp"]
    fine = Mesh(mesh.devices.reshape(RINGS, ctx_count // SLOTS, 2, fsdp_count), ALL)
    tokens = P("fsdp", CTX, None)
    states = P(ALL, None)
    return jax.shard_map(
        on_device,
        mesh=fine,
        in_specs=(
            tokens,
            tokens,
            P("fsdp", None),
            P("fsdp", None, None),
            P("fsdp", CTX),
            *([states] * 6),
            *([P()] * 3),
        ),
        out_specs=(tokens, tokens, *([states] * 6), *([P()] * 3)),
        check_vma=False,
    )
```
